512 devices in a mesh: ia: 32 (over z, core), ja: 4 (over y), ka: 4 (over x).
Axes of the slice: x: 4, y: 4, z: 16, core: 2. Of those that a mesh axis runs over, the one named last changes fastest.
Arguments:
- tensor: float32 [512, 1024, 512], P('ia', 'ja', 'ka'), may hold values from -75 to 75
- second_factor: float32 [4, 256, 24], P('ja', 'ia'), may hold values from -0.79549513 to 0.79549513
- third_factor: float32 [4, 128, 24], P('ka', 'ia'), may hold values from -1.125 to 1.125
Outputs:
- factor: float32 [512, 24], P('ia')
- column_rms: float32 [24], replicated
- correlation: float32 [24, 24], replicated
The draws below stay inside these ranges and needn't reach their ends.
All inputs are finite; a program needn't handle non-finite values.
Results may differ from the reference program's by a relative error of at most 0.0003.
Values sent between devices are 32-bit elements; how exact they have to be, the bound alone decides.
No kernel may reach another device: no remote copies, remote signals or barrier semaphores. Data moves between devices by JAX's collectives and lax.ppermute only.
A program may use at most 64 MiB of HBM per device.

```python
import math
import jax
import jax.numpy as jnp
from jax import lax

RANK = 24
I_DEV = 16
J_DEV = 256
K_DEV = 128
I_LEN = 512
J_LEN = 1024
K_LEN = 512
N_IA = 32


def draw_tensor(key, part):
    key = jax.random.fold_in(key, 5)
    key_cell, key_row = jax.random.split(key, 2)
    position = jnp.arange(I_LEN, dtype=jnp.float32) / I_LEN
    cells = jax.random.truncated_normal(key_cell, -5.0, 5.0, (I_LEN, J_LEN, K_LEN), jnp.float32)
    rising = 3.0 ** position
    scales = jnp.exp(jax.random.uniform(key_row, (I_LEN,), jnp.float32, math.log(0.3), math.log(3.0)))
    return cells * (scales * rising)[:, None, None]


def draw_second_factor(key, part):
    key = jax.random.fold_in(key, 11)
    key_row, key_own, key_col = jax.random.split(key, 3)
    common = jax.random.truncated_normal(key_row, -3.0, 3.0, (J_LEN, 1), jnp.float32)
    own = jax.random.truncated_normal(key_own, -3.0, 3.0, (J_LEN, RANK), jnp.float32)
    spread = jnp.exp(jax.random.uniform(key_col, (1, RANK), jnp.float32, math.log(0.5), math.log(2.0)))
    rising = 3.0 ** (jnp.arange(J_LEN, dtype=jnp.float32)[:, None] / J_LEN)
    rows = (common + own) * spread * rising / math.sqrt(2.0 * J_LEN)
    return rows.reshape(J_LEN // J_DEV, J_DEV, RANK)


def draw_third_factor(key, part):
    key = jax.random.fold_in(key, 13)
    key_row, key_own, key_col = jax.random.split(key, 3)
    common = jax.random.truncated_normal(key_row, -3.0, 3.0, (K_LEN, 1), jnp.float32)
    own = jax.random.truncated_normal(key_own, -3.0, 3.0, (K_LEN, RANK), jnp.float32)
    spread = jnp.exp(jax.random.uniform(key_col, (1, RANK), jnp.float32, math.log(0.5), math.log(2.0)))
    rising = 3.0 ** (jnp.arange(K_LEN, dtype=jnp.float32)[:, None] / K_LEN)
    rows = (common + own) * spread * rising / math.sqrt(2.0 * K_LEN)
    return rows.reshape(K_LEN // K_DEV, K_DEV, RANK)


def setup_inputs(seed: int = 0) -> dict:
    seeds = jax.random.split(jax.random.key(seed), 4)
    return {
        "tensor": draw_tensor(jax.random.fold_in(seeds[3], 71), 0),
        "second_factor": draw_second_factor(jax.random.fold_in(seeds[3], 71), 0),
        "third_factor": draw_third_factor(jax.random.fold_in(seeds[3], 71), 0),
    }


EPSILON = 1e-06

def gram_of(row_block):
    return jnp.dot(row_block.T.astype(jnp.float32), row_block.astype(jnp.float32), precision=lax.Precision.HIGHEST, preferred_element_type=jnp.float32)

def solve_rows(system, row_block):
    lower_factor = jnp.linalg.cholesky(system)
    return jax.scipy.linalg.cho_solve((lower_factor, True), row_block.T).T

def reference(tensor, second_factor, third_factor):
    highest = lax.Precision.HIGHEST
    width_rank = second_factor.shape[-1]
    rows_two = second_factor.reshape(-1, width_rank)
    rows_three = third_factor.reshape(-1, width_rank)
    system = gram_of(rows_two) * gram_of(rows_three)
    slabs = tensor.reshape(N_IA, I_DEV, J_LEN, K_LEN)

    def contract(slab_rows):
        through = jnp.einsum('ijk,kr->rij', slab_rows.astype(jnp.float32), rows_three.astype(jnp.float32), precision=highest, preferred_element_type=jnp.float32)
        return jnp.einsum('rij,jr->ir', through.astype(jnp.float32), rows_two.astype(jnp.float32), precision=highest, preferred_element_type=jnp.float32)
    product = lax.map(contract, slabs).reshape(I_LEN, width_rank)
    updated = solve_rows(system, product)
    gram_first = gram_of(updated)
    column_rms = jnp.sqrt(jnp.diagonal(gram_first) / I_LEN + EPSILON)
    factor = updated / column_rms[None, :]
    correlation = gram_first / (column_rms[:, None] * column_rms[None, :]) / I_LEN
    return (factor, column_rms, correlation)
```

```python
import jax
import jax.numpy as jnp
from jax import lax
from jax.sharding import PartitionSpec as P

EPSILON = 1e-06


def gram_of(row_block):
    return jnp.dot(
        row_block.T, row_block, precision=lax.Precision.HIGHEST, preferred_element_type=jnp.float32
    )


def solve_rows(system, row_block):
    lower_factor = jnp.linalg.cholesky(system)
    return jax.scipy.linalg.cho_solve((lower_factor, True), row_block.T).T


def exchange(flat, axes):
    count = lax.axis_size(axes)
    return lax.all_to_all(jnp.broadcast_to(flat[None], (count,) + flat.shape), axes, 0, 0, tiled=True)


def per_device(tensor, second_factor, third_factor):
    highest = lax.Precision.HIGHEST
    rank = second_factor.shape[-1]
    own_two, own_three = second_factor[0], third_factor[0]
    local_rows = tensor.shape[0]
    total_rows = local_rows * lax.axis_size("ia")

    packed = jnp.concatenate([own_two.reshape(-1), own_three.reshape(-1)])
    gathered = exchange(packed, "ia")
    rows_two = gathered[:, : own_two.size].reshape(-1, rank)
    rows_three = gathered[:, own_two.size :].reshape(-1, rank)

    through = jnp.einsum(
        "ijk,kr->ijr", tensor, rows_three, precision=highest, preferred_element_type=jnp.float32
    )
    partial = jnp.sum(through * rows_two[None], axis=1)
    message = jnp.concatenate([partial, gram_of(rows_two), gram_of(rows_three)], axis=0)
    parts = exchange(message.reshape(-1), ("ja", "ka"))
    scale_two, scale_three = 1.0 / lax.axis_size("ka"), 1.0 / lax.axis_size("ja")
    total = jnp.sum(parts, axis=0).reshape(-1, rank)
    summed = total[:local_rows]
    gram_two = total[local_rows : local_rows + rank] * scale_two
    gram_three = total[local_rows + rank :] * scale_three
    updated = solve_rows(gram_two * gram_three, summed)

    grams = exchange(gram_of(updated).reshape(-1), "ia")
    gram_first = jnp.sum(grams, axis=0).reshape(rank, rank)
    column_rms = jnp.sqrt(jnp.diagonal(gram_first) / total_rows + EPSILON)
    factor = updated / column_rms[None, :]
    correlation = gram_first / (column_rms[:, None] * column_rms[None, :]) / total_rows
    return (factor, column_rms, correlation)


def solution(mesh):
    return jax.shard_map(
        per_device,
        mesh=mesh,
        in_specs=(P("ia", "ja", "ka"), P("ja", "ia", None), P("ka", "ia", None)),
        out_specs=(P("ia", None), P(), P()),
        check_vma=False,
    )
```

```python
import functools

import jax
import jax.numpy as jnp
from jax import lax
from jax.experimental import pallas as pl
from jax.experimental.pallas import tpu as pltpu
from jax.sharding import Mesh, PartitionSpec as P

EPSILON = 1e-06
LANES = 128
SUBLANES = 8
BLOCK = 12


def exchange(copies, axes):
    return lax.all_to_all(copies, axes, 0, 0, tiled=True)


def lane_start(slot, rank):
    per_tile = LANES // rank
    return LANES * (slot // per_tile) + rank * (slot % per_tile)


def call(kernel, out_shape, scratch, *operands):
    vmem = pl.BlockSpec(memory_space=pltpu.VMEM)
    return pl.pallas_call(
        kernel,
        out_shape=out_shape,
        in_specs=[vmem] * len(operands),
        out_specs=jax.tree.map(lambda _: vmem, out_shape),
        scratch_shapes=scratch,
    )(*operands)


def pack_kernel(two_ref, three_ref, out_ref):
    rank = two_ref.shape[-1]
    rows = [two_ref[0, r : r + 1, :] for r in range(two_ref.shape[1])]
    rows += [three_ref[0, r : r + 1, :] for r in range(three_ref.shape[1])]
    pieces, at = [], 0
    for slot, row in enumerate(rows):
        start = lane_start(slot, rank)
        if start > at:
            pieces.append(jnp.zeros((1, start - at), jnp.float32))
        pieces.append(row)
        at = start + rank
    pieces.append(jnp.zeros((1, out_ref.shape[-1] - at), jnp.float32))
    out_ref[...] = jnp.broadcast_to(jnp.concatenate(pieces, axis=1), out_ref.shape)


def parts_of(thrice, rank):
    high = thrice.astype(jnp.bfloat16).astype(jnp.float32)
    rest = thrice - high
    middle = rest.astype(jnp.bfloat16).astype(jnp.float32)
    lane = lax.broadcasted_iota(jnp.int32, thrice.shape, 1)
    return jnp.where(
        lane < rank, high, jnp.where(lane < 2 * rank, middle, rest - middle)
    ).astype(jnp.bfloat16)


def fold_lanes(wide, rank):
    return wide[:, :rank] + wide[:, rank : 2 * rank] + wide[:, 2 * rank : 3 * rank]


def fold_gram(full, rank):
    return fold_lanes(full[:rank] + full[rank : 2 * rank] + full[2 * rank : 3 * rank], rank)


def gram_of_parts(parts, rank):
    full = lax.dot_general(
        parts, parts, (((0,), (0,)), ((), ())), preferred_element_type=jnp.float32
    )
    return fold_gram(full, rank)


def contract_kernel(
    gathered_ref, tensor_ref, out_ref, two_ref, three_ref, sums_ref, gram_two_ref, gram_three_ref,
    *, rank, cores, chips
):
    count_two = two_ref.shape[0] // (cores * chips)
    count_three = three_ref.shape[0] // (cores * chips)
    for core in range(cores):
        block = gathered_ref[core * chips : (core + 1) * chips, :]
        for slot in range(count_two + count_three):
            start = lane_start(slot, rank)
            piece = block[:, start : start + rank]
            thrice = jnp.concatenate([piece, piece, piece], axis=1)
            if slot < count_two:
                two_ref[pl.ds(count_two * core + slot, chips, stride=count_two * cores), :] = thrice
            else:
                first = count_three * core + slot - count_two
                three_ref[pl.ds(first, chips, stride=count_three * cores), :] = thrice
    two = two_ref[...]
    parts_three = parts_of(three_ref[...], rank)
    double = jnp.concatenate([parts_three, parts_three], axis=0)
    for row in range(tensor_ref.shape[0]):
        cells = tensor_ref[row]
        high = cells.astype(jnp.bfloat16)
        rest = cells - high.astype(jnp.float32)
        middle = rest.astype(jnp.bfloat16)
        low = (rest - middle.astype(jnp.float32)).astype(jnp.bfloat16)
        through = jnp.dot(
            jnp.concatenate([high, middle], axis=1), double, preferred_element_type=jnp.float32
        )
        through += jnp.dot(low, parts_three, preferred_element_type=jnp.float32)
        sums_ref[row : row + 1, :] = jnp.sum(through * two, axis=0, keepdims=True)
    partial = fold_lanes(sums_ref[...], rank).T
    gram_two_ref[...] = gram_of_parts(parts_of(two, rank), rank)
    gram_three_ref[...] = gram_of_parts(parts_three, rank)
    tiles = rank // SUBLANES
    tile_two = SUBLANES * jnp.minimum(lax.axis_index("ka"), tiles - 1)
    tile_three = SUBLANES * jnp.minimum(lax.axis_index("ja"), tiles - 1)
    pieces = [partial[SUBLANES * t : SUBLANES * (t + 1)] for t in range(tiles)]
    pieces.append(gram_two_ref[pl.ds(pl.multiple_of(tile_two, SUBLANES), SUBLANES), :])
    pieces.append(gram_three_ref[pl.ds(pl.multiple_of(tile_three, SUBLANES), SUBLANES), :])
    out_ref[...] = jnp.broadcast_to(jnp.concatenate(pieces, axis=1)[None], out_ref.shape)


def across_sublanes(tile, sublane):
    return jnp.broadcast_to(tile[sublane : sublane + 1, :], tile.shape)


def across_lanes(tile, lane):
    return jnp.broadcast_to(tile[:, lane : lane + 1], tile.shape)


def eliminate(tiles, rank):
    sublane = lax.broadcasted_iota(jnp.int32, tiles[0].shape, 0)

    def reduced(values, column, pivot_row, pivot_tile, pivot_sublane):
        out = [v - c * pivot_row for v, c in zip(values, column)]
        out[pivot_tile] = jnp.where(sublane == pivot_sublane, pivot_row, out[pivot_tile])
        return out

    for begin in range(0, rank, BLOCK):
        columns = [[across_lanes(v, begin + m) for v in tiles] for m in range(BLOCK)]
        for m in range(BLOCK):
            t, s = divmod(begin + m, SUBLANES)
            column = columns[m]
            inverse = 1.0 / across_sublanes(column[t], s)
            pivot_row = across_sublanes(tiles[t], s) * inverse
            tiles = reduced(tiles, column, pivot_row, t, s)
            for later in range(m + 1, BLOCK):
                entry = across_sublanes(columns[later][t], s) * inverse
                columns[later] = reduced(columns[later], column, entry, t, s)
    return tiles


def solve_kernel(parts_ref, out_ref, updated_ref, *, rank, rows, cores, groups_two, groups_three):
    tiles = rank // SUBLANES
    group = groups_two * groups_three
    products = []
    for core in range(cores):
        total = parts_ref[core * group]
        for source in range(1, group):
            total += parts_ref[core * group + source]
        products.append(total)
    at_two, at_three = tiles * rows, tiles * rows + rank
    augmented = []
    for t in range(tiles):
        gram_two = parts_ref[t]
        for j in range(1, groups_two):
            gram_two += parts_ref[j * groups_three + t]
        gram_three = parts_ref[t * groups_three]
        for k in range(1, groups_three):
            gram_three += parts_ref[t * groups_three + k]
        system = gram_two[:, at_two : at_two + rank] * gram_three[:, at_three : at_three + rank]
        sides = [product[:, rows * t : rows * (t + 1)] for product in products]
        augmented.append(jnp.concatenate([system] + sides, axis=1))
    solved = jnp.concatenate([v[:, rank:] for v in eliminate(augmented, rank)], axis=0)
    updated_ref[...] = solved
    high = solved.astype(jnp.bfloat16)
    rest = solved - high.astype(jnp.float32)
    middle = rest.astype(jnp.bfloat16)
    low = (rest - middle.astype(jnp.float32)).astype(jnp.bfloat16)
    stacked = jnp.concatenate([high, middle, low], axis=0)
    full = lax.dot_general(
        stacked, stacked, (((1,), (1,)), ((), ())), preferred_element_type=jnp.float32
    )
    gram = fold_gram(full, rank)
    pieces = [gram[SUBLANES * t : SUBLANES * (t + 1)] for t in range(tiles)]
    out_ref[...] = jnp.broadcast_to(jnp.concatenate(pieces, axis=1)[None], out_ref.shape)


def scale_kernel(grams_ref, updated_ref, factor_ref, rms_ref, correlation_ref, *, rank, total_rows):
    total = grams_ref[0]
    for source in range(1, grams_ref.shape[0]):
        total += grams_ref[source]
    gram = jnp.concatenate(
        [total[:, rank * t : rank * (t + 1)] for t in range(rank // SUBLANES)], axis=0
    )
    diagonal = jnp.where(
        lax.broadcasted_iota(jnp.int32, gram.shape, 0) == lax.broadcasted_iota(jnp.int32, gram.shape, 1),
        gram,
        0.0,
    )
    rms_row = jnp.sqrt(jnp.sum(diagonal, axis=0, keepdims=True) / total_rows + EPSILON)
    rms_column = jnp.sqrt(jnp.sum(diagonal, axis=1, keepdims=True) / total_rows + EPSILON)
    rms_ref[...] = rms_row
    factor_ref[...] = updated_ref[...] / rms_row
    correlation_ref[...] = gram / (rms_column * rms_row) / total_rows


def per_device(tensor, second_factor, third_factor):
    f32 = jnp.float32
    rank = second_factor.shape[-1]
    chips, cores = lax.axis_size("z"), lax.axis_size("core")
    groups_two, groups_three = lax.axis_size("ja"), lax.axis_size("ka")
    members = chips * cores
    rows = tensor.shape[0]
    total_rows = rows * members
    slots = second_factor.shape[1] + third_factor.shape[1]
    width = -(-(lane_start(slots - 1, rank) + rank) // LANES) * LANES
    tiles = rank // SUBLANES

    packed = call(
        pack_kernel, jax.ShapeDtypeStruct((members, width), f32), [], second_factor, third_factor
    )
    gathered = exchange(packed, ("core", "z"))

    messages = call(
        functools.partial(contract_kernel, rank=rank, cores=cores, chips=chips),
        jax.ShapeDtypeStruct((cores * groups_two * groups_three, SUBLANES, tiles * rows + 2 * rank), f32),
        [
            pltpu.VMEM((tensor.shape[1], 3 * rank), f32),
            pltpu.VMEM((tensor.shape[2], 3 * rank), f32),
            pltpu.VMEM((rows, 3 * rank), f32),
            pltpu.VMEM((rank, rank), f32),
            pltpu.VMEM((rank, rank), f32),
        ],
        gathered,
        tensor,
    )
    parts = exchange(messages, ("core", "ja", "ka"))

    grams, solved = call(
        functools.partial(
            solve_kernel, rank=rank, rows=rows, cores=cores, groups_two=groups_two, groups_three=groups_three
        ),
        (
            jax.ShapeDtypeStruct((chips, SUBLANES, tiles * rank), f32),
            jax.ShapeDtypeStruct((rank, cores * rows), f32),
        ),
        [],
        parts,
    )
    grams = exchange(grams, "z")
    updated = lax.dynamic_slice_in_dim(solved.T, lax.axis_index("core") * rows, rows, 0)

    factor, column_rms, correlation = call(
        functools.partial(scale_kernel, rank=rank, total_rows=total_rows),
        (
            jax.ShapeDtypeStruct((rows, rank), f32),
            jax.ShapeDtypeStruct((1, rank), f32),
            jax.ShapeDtypeStruct((rank, rank), f32),
        ),
        [],
        grams,
        updated,
    )
    return (factor, column_rms[0], correlation)


def solution(mesh):
    ia, ja, ka = (mesh.shape[name] for name in ("ia", "ja", "ka"))
    split = Mesh(mesh.devices.reshape(ia // 2, 2, ja, ka), ("z", "core", "ja", "ka"))
    first = ("z", "core")
    return jax.shard_map(
        per_device,
        mesh=split,
        in_specs=(P(first, "ja", "ka"), P("ja", first, None), P("ka", first, None)),
        out_specs=(P(first, None), P(), P()),
        check_vma=False,
    )
```

```python
import functools

import jax
import jax.numpy as jnp
from jax import lax
from jax.experimental import pallas as pl
from jax.experimental.pallas import tpu as pltpu
from jax.sharding import Mesh, PartitionSpec as P

EPSILON = 1e-06
LANES = 128
SUBLANES = 8
BLOCK = 12
VMEM_BYTES = 8 * 2**20


def exchange(copies, axes):
    return lax.all_to_all(copies, axes, 0, 0, tiled=True)


def lane_start(slot, rank):
    per_tile = LANES // rank
    return LANES * (slot // per_tile) + rank * (slot % per_tile)


def call(kernel, out_shape, scratch, *operands, fetched=(), cost=None):
    vmem, hbm = pl.BlockSpec(memory_space=pltpu.VMEM), pl.BlockSpec(memory_space=pltpu.HBM)
    return pl.pallas_call(
        kernel,
        out_shape=out_shape,
        in_specs=[hbm if at in fetched else vmem for at in range(len(operands))],
        out_specs=jax.tree.map(lambda _: vmem, out_shape),
        scratch_shapes=scratch,
        cost_estimate=cost,
        compiler_params=pltpu.CompilerParams(vmem_limit_bytes=VMEM_BYTES),
    )(*operands)


def pack_kernel(two_hbm, three_hbm, out_ref, two_ref, three_ref, arrived):
    copies = [
        pltpu.make_async_copy(two_hbm, two_ref, arrived.at[0]),
        pltpu.make_async_copy(three_hbm, three_ref, arrived.at[1]),
    ]
    for copy in copies:
        copy.start()
    for copy in copies:
        copy.wait()
    rank = two_ref.shape[-1]
    rows = [two_ref[0, r : r + 1, :] for r in range(two_ref.shape[1])]
    rows += [three_ref[0, r : r + 1, :] for r in range(three_ref.shape[1])]
    pieces, at = [], 0
    for slot, row in enumerate(rows):
        start = lane_start(slot, rank)
        if start > at:
            pieces.append(jnp.zeros((1, start - at), jnp.float32))
        pieces.append(row)
        at = start + rank
    pieces.append(jnp.zeros((1, out_ref.shape[-1] - at), jnp.float32))
    out_ref[...] = jnp.broadcast_to(jnp.concatenate(pieces, axis=1)[None], out_ref.shape)


def parts_of(thrice, rank):
    high = thrice.astype(jnp.bfloat16).astype(jnp.float32)
    rest = thrice - high
    middle = rest.astype(jnp.bfloat16).astype(jnp.float32)
    lane = lax.broadcasted_iota(jnp.int32, thrice.shape, 1)
    return jnp.where(
        lane < rank, high, jnp.where(lane < 2 * rank, middle, rest - middle)
    ).astype(jnp.bfloat16)


def fold_lanes(wide, rank):
    return wide[:, :rank] + wide[:, rank : 2 * rank] + wide[:, 2 * rank : 3 * rank]


def fold_gram(full, rank):
    return fold_lanes(full[:rank] + full[rank : 2 * rank] + full[2 * rank : 3 * rank], rank)


def gram_of_parts(parts, rank):
    full = lax.dot_general(
        parts, parts, (((0,), (0,)), ((), ())), preferred_element_type=jnp.float32
    )
    return fold_gram(full, rank)


def split_kernel(tensor_ref, upper_ref, low_ref):
    width = tensor_ref.shape[-1]

    @pl.loop(0, tensor_ref.shape[0])
    def _(row):
        cells = tensor_ref[row]
        high = cells.astype(jnp.bfloat16)
        rest = cells - high.astype(jnp.float32)
        middle = rest.astype(jnp.bfloat16)
        upper_ref[row, :, :width] = high
        upper_ref[row, :, width:] = middle
        low_ref[row] = (rest - middle.astype(jnp.float32)).astype(jnp.bfloat16)


def contract_kernel(
    gathered_ref, upper_ref, low_ref, out_ref, two_ref, three_ref, sums_ref,
    gram_two_ref, gram_three_ref, *, rank, cores, chips
):
    count_two = two_ref.shape[0] // (cores * chips)
    count_three = three_ref.shape[0] // (cores * chips)
    for core in range(cores):
        block = gathered_ref[core * chips : (core + 1) * chips, :]
        for slot in range(count_two + count_three):
            start = lane_start(slot, rank)
            piece = block[:, start : start + rank]
            thrice = jnp.concatenate([piece, piece, piece], axis=1)
            if slot < count_two:
                two_ref[pl.ds(count_two * core + slot, chips, stride=count_two * cores), :] = thrice
            else:
                first = count_three * core + slot - count_two
                three_ref[pl.ds(first, chips, stride=count_three * cores), :] = thrice
    two = two_ref[...]
    parts_three = parts_of(three_ref[...], rank)
    double = jnp.concatenate([parts_three, parts_three], axis=0)
    for row in range(upper_ref.shape[0]):
        through = jnp.dot(upper_ref[row], double, preferred_element_type=jnp.float32)
        through += jnp.dot(low_ref[row], parts_three, preferred_element_type=jnp.float32)
        sums_ref[row : row + 1, :] = jnp.sum(through * two, axis=0, keepdims=True)
    partial = fold_lanes(sums_ref[...], rank).T
    gram_two_ref[...] = gram_of_parts(parts_of(two, rank), rank)
    gram_three_ref[...] = gram_of_parts(parts_three, rank)
    tiles = rank // SUBLANES
    tile_two = SUBLANES * jnp.minimum(lax.axis_index("ka"), tiles - 1)
    tile_three = SUBLANES * jnp.minimum(lax.axis_index("ja"), tiles - 1)
    pieces = [partial[SUBLANES * t : SUBLANES * (t + 1)] for t in range(tiles)]
    pieces.append(gram_two_ref[pl.ds(pl.multiple_of(tile_two, SUBLANES), SUBLANES), :])
    pieces.append(gram_three_ref[pl.ds(pl.multiple_of(tile_three, SUBLANES), SUBLANES), :])
    out_ref[...] = jnp.broadcast_to(jnp.concatenate(pieces, axis=1)[None], out_ref.shape)


def across_sublanes(tile, sublane):
    return jnp.broadcast_to(tile[sublane : sublane + 1, :], tile.shape)


def across_lanes(tile, lane):
    return jnp.broadcast_to(tile[:, lane : lane + 1], tile.shape)


def eliminate(tiles, rank):
    sublane = lax.broadcasted_iota(jnp.int32, tiles[0].shape, 0)

    def reduced(values, column, pivot_row, pivot_tile, pivot_sublane):
        out = [v - c * pivot_row for v, c in zip(values, column)]
        out[pivot_tile] = jnp.where(sublane == pivot_sublane, pivot_row, out[pivot_tile])
        return out

    for begin in range(0, rank, BLOCK):
        columns = [[across_lanes(v, begin + m) for v in tiles] for m in range(BLOCK)]
        for m in range(BLOCK):
            t, s = divmod(begin + m, SUBLANES)
            column = columns[m]
            inverse = 1.0 / across_sublanes(column[t], s)
            pivot_row = across_sublanes(tiles[t], s) * inverse
            tiles = reduced(tiles, column, pivot_row, t, s)
            for later in range(m + 1, BLOCK):
                entry = across_sublanes(columns[later][t], s) * inverse
                columns[later] = reduced(columns[later], column, entry, t, s)
    return tiles


def solve_kernel(parts_ref, out_ref, updated_ref, chip_ref, *, rank, rows, cores, groups_two, groups_three):
    tiles = rank // SUBLANES
    group = groups_two * groups_three
    products = []
    for core in range(cores):
        total = parts_ref[core * group]
        for source in range(1, group):
            total += parts_ref[core * group + source]
        products.append(total)
    at_two, at_three = tiles * rows, tiles * rows + rank
    augmented = []
    for t in range(tiles):
        gram_two = parts_ref[t]
        for j in range(1, groups_two):
            gram_two += parts_ref[j * groups_three + t]
        gram_three = parts_ref[t * groups_three]
        for k in range(1, groups_three):
            gram_three += parts_ref[t * groups_three + k]
        system = gram_two[:, at_two : at_two + rank] * gram_three[:, at_three : at_three + rank]
        sides = [product[:, rows * t : rows * (t + 1)] for product in products]
        augmented.append(jnp.concatenate([system] + sides, axis=1))
    solved = jnp.concatenate([v[:, rank:] for v in eliminate(augmented, rank)], axis=0)
    chip_ref[...] = solved.T
    first = pl.multiple_of(rows * lax.axis_index("core"), SUBLANES)
    updated_ref[...] = chip_ref[pl.ds(first, rows), :]
    high = solved.astype(jnp.bfloat16)
    rest = solved - high.astype(jnp.float32)
    middle = rest.astype(jnp.bfloat16)
    low = (rest - middle.astype(jnp.float32)).astype(jnp.bfloat16)
    stacked = jnp.concatenate([high, middle, low], axis=0)
    full = lax.dot_general(
        stacked, stacked, (((1,), (1,)), ((), ())), preferred_element_type=jnp.float32
    )
    gram = fold_gram(full, rank)
    pieces = [gram[SUBLANES * t : SUBLANES * (t + 1)] for t in range(tiles)]
    out_ref[...] = jnp.broadcast_to(jnp.concatenate(pieces, axis=1)[None], out_ref.shape)


def scale_kernel(grams_ref, updated_ref, factor_ref, rms_ref, correlation_ref, *, rank, total_rows):
    total = grams_ref[0]
    for source in range(1, grams_ref.shape[0]):
        total += grams_ref[source]
    gram = jnp.concatenate(
        [total[:, rank * t : rank * (t + 1)] for t in range(rank // SUBLANES)], axis=0
    )
    diagonal = jnp.where(
        lax.broadcasted_iota(jnp.int32, gram.shape, 0) == lax.broadcasted_iota(jnp.int32, gram.shape, 1),
        gram,
        0.0,
    )
    rms_row = jnp.sqrt(jnp.sum(diagonal, axis=0, keepdims=True) / total_rows + EPSILON)
    rms_column = jnp.sqrt(jnp.sum(diagonal, axis=1, keepdims=True) / total_rows + EPSILON)
    rms_ref[...] = rms_row
    factor_ref[...] = updated_ref[...] / rms_row
    correlation_ref[...] = gram / (rms_column * rms_row) / total_rows


def per_device(tensor, second_factor, third_factor):
    f32 = jnp.float32
    second_factor, third_factor = (
        pltpu.with_memory_space_constraint(v, pltpu.HBM) for v in (second_factor, third_factor)
    )
    rank = second_factor.shape[-1]
    chips, cores = lax.axis_size("z"), lax.axis_size("core")
    groups_two, groups_three = lax.axis_size("ja"), lax.axis_size("ka")
    members = chips * cores
    rows = tensor.shape[0]
    total_rows = rows * members
    slots = second_factor.shape[1] + third_factor.shape[1]
    width = -(-(lane_start(slots - 1, rank) + rank) // LANES) * LANES
    tiles = rank // SUBLANES

    packed = call(
        pack_kernel,
        jax.ShapeDtypeStruct((members, 1, width), f32),
        [
            pltpu.VMEM(second_factor.shape, f32),
            pltpu.VMEM(third_factor.shape, f32),
            pltpu.SemaphoreType.DMA((2,)),
        ],
        second_factor,
        third_factor,
        fetched=(0, 1),
    )
    gathered = exchange(packed, ("core", "z")).reshape(members, width)

    upper, low = call(
        split_kernel,
        (
            jax.ShapeDtypeStruct((*tensor.shape[:2], 2 * tensor.shape[2]), jnp.bfloat16),
            jax.ShapeDtypeStruct(tensor.shape, jnp.bfloat16),
        ),
        [],
        tensor,
        cost=pl.CostEstimate(flops=5 * tensor.size, bytes_accessed=10 * tensor.size, transcendentals=0),
    )
    messages = call(
        functools.partial(contract_kernel, rank=rank, cores=cores, chips=chips),
        jax.ShapeDtypeStruct((cores * groups_two * groups_three, SUBLANES, tiles * rows + 2 * rank), f32),
        [
            pltpu.VMEM((tensor.shape[1], 3 * rank), f32),
            pltpu.VMEM((tensor.shape[2], 3 * rank), f32),
            pltpu.VMEM((rows, 3 * rank), f32),
            pltpu.VMEM((rank, rank), f32),
            pltpu.VMEM((rank, rank), f32),
        ],
        gathered,
        upper,
        low,
    )
    parts = exchange(messages, ("core", "ja", "ka"))

    grams, updated = call(
        functools.partial(
            solve_kernel, rank=rank, rows=rows, cores=cores, groups_two=groups_two, groups_three=groups_three
        ),
        (
            jax.ShapeDtypeStruct((chips, SUBLANES, tiles * rank), f32),
            jax.ShapeDtypeStruct((rows, rank), f32),
        ),
        [pltpu.VMEM((cores * rows, rank), f32)],
        parts,
    )
    grams = exchange(grams, "z")

    factor, column_rms, correlation = call(
        functools.partial(scale_kernel, rank=rank, total_rows=total_rows),
        (
            jax.ShapeDtypeStruct((rows, rank), f32),
            jax.ShapeDtypeStruct((1, rank), f32),
            jax.ShapeDtypeStruct((rank, rank), f32),
        ),
        [],
        grams,
        updated,
    )
    return (factor, column_rms[0], correlation)


def solution(mesh):
    ia, ja, ka = (mesh.shape[name] for name in ("ia", "ja", "ka"))
    split = Mesh(mesh.devices.reshape(ia // 2, 2, ja, ka), ("z", "core", "ja", "ka"))
    first = ("z", "core")
    return jax.shard_map(
        per_device,
        mesh=split,
        in_specs=(P(first, "ja", "ka"), P("ja", first, None), P("ka", first, None)),
        out_specs=(P(first, None), P(), P()),
        check_vma=False,
    )
```

```python
import functools
import itertools

import jax
import jax.numpy as jnp
import numpy as np
from jax import lax
from jax.experimental import pallas as pl
from jax.experimental.pallas import tpu as pltpu
from jax.sharding import Mesh, PartitionSpec as P

EPSILON = 1e-06
LANES = 128
SUBLANES = 8
BLOCK = 12
VMEM_BYTES = 8 * 2**20


def counted_from(start, size):
    return [(start + step) % size for step in range(size)]


def exchange(copies, axes, starts):
    sizes = [lax.axis_size(axis) for axis in axes]
    order = [
        int(np.ravel_multi_index(member, sizes))
        for member in itertools.product(*map(counted_from, starts, sizes))
    ]
    return lax.all_to_all(copies, axes, 0, 0, tiled=True, axis_index_groups=[order])


def lane_start(slot, rank):
    per_tile = LANES // rank
    return LANES * (slot // per_tile) + rank * (slot % per_tile)


def call(kernel, out_shape, scratch, *operands, fetched=(), cost=None):
    vmem, hbm = pl.BlockSpec(memory_space=pltpu.VMEM), pl.BlockSpec(memory_space=pltpu.HBM)
    return pl.pallas_call(
        kernel,
        out_shape=out_shape,
        in_specs=[hbm if at in fetched else vmem for at in range(len(operands))],
        out_specs=jax.tree.map(lambda _: vmem, out_shape),
        scratch_shapes=scratch,
        cost_estimate=cost,
        compiler_params=pltpu.CompilerParams(vmem_limit_bytes=VMEM_BYTES),
    )(*operands)


def pack_kernel(two_hbm, three_hbm, out_ref, two_ref, three_ref, arrived):
    copies = [
        pltpu.make_async_copy(two_hbm, two_ref, arrived.at[0]),
        pltpu.make_async_copy(three_hbm, three_ref, arrived.at[1]),
    ]
    for copy in copies:
        copy.start()
    for copy in copies:
        copy.wait()
    rank = two_ref.shape[-1]
    rows = [two_ref[0, r : r + 1, :] for r in range(two_ref.shape[1])]
    rows += [three_ref[0, r : r + 1, :] for r in range(three_ref.shape[1])]
    pieces, at = [], 0
    for slot, row in enumerate(rows):
        start = lane_start(slot, rank)
        if start > at:
            pieces.append(jnp.zeros((1, start - at), jnp.float32))
        pieces.append(row)
        at = start + rank
    pieces.append(jnp.zeros((1, out_ref.shape[-1] - at), jnp.float32))
    out_ref[...] = jnp.broadcast_to(jnp.concatenate(pieces, axis=1)[None], out_ref.shape)


def parts_of(thrice, rank):
    high = thrice.astype(jnp.bfloat16).astype(jnp.float32)
    rest = thrice - high
    middle = rest.astype(jnp.bfloat16).astype(jnp.float32)
    lane = lax.broadcasted_iota(jnp.int32, thrice.shape, 1)
    return jnp.where(
        lane < rank, high, jnp.where(lane < 2 * rank, middle, rest - middle)
    ).astype(jnp.bfloat16)


def fold_lanes(wide, rank):
    return wide[:, :rank] + wide[:, rank : 2 * rank] + wide[:, 2 * rank : 3 * rank]


def fold_gram(full, rank):
    return fold_lanes(full[:rank] + full[rank : 2 * rank] + full[2 * rank : 3 * rank], rank)


def gram_of_parts(parts, rank):
    full = lax.dot_general(
        parts, parts, (((0,), (0,)), ((), ())), preferred_element_type=jnp.float32
    )
    return fold_gram(full, rank)


def split_kernel(tensor_ref, upper_ref, low_ref):
    width = tensor_ref.shape[-1]

    @pl.loop(0, tensor_ref.shape[0])
    def _(row):
        cells = tensor_ref[row]
        high = cells.astype(jnp.bfloat16)
        rest = cells - high.astype(jnp.float32)
        middle = rest.astype(jnp.bfloat16)
        upper_ref[row, :, :width] = high
        upper_ref[row, :, width:] = middle
        low = (rest - middle.astype(jnp.float32)).astype(jnp.bfloat16)
        half = tensor_ref.shape[0] // 2

        @pl.when(row < half)
        def _():
            low_ref[row, :, :width] = low

        @pl.when(row >= half)
        def _():
            low_ref[row - half, :, width:] = low


def runs_from(start, size):
    return [(0, start, size - start)] + ([(size - start, 0, start)] if start else [])


def contract_kernel(
    gathered_ref, upper_ref, low_ref, out_ref, two_ref, three_ref, sums_ref,
    gram_two_ref, gram_three_ref, *, rank, cores, chips, starts
):
    count_two = two_ref.shape[0] // (cores * chips)
    count_three = three_ref.shape[0] // (cores * chips)
    for at, core in enumerate(counted_from(starts[0], cores)):
        for first, chip, run in runs_from(starts[1], chips):
            block = gathered_ref[at * chips + first : at * chips + first + run, :]
            for slot in range(count_two + count_three):
                start = lane_start(slot, rank)
                piece = block[:, start : start + rank]
                thrice = jnp.concatenate([piece, piece, piece], axis=1)
                ref, count, row = (
                    (two_ref, count_two, slot) if slot < count_two else (three_ref, count_three, slot - count_two)
                )
                row += count * (cores * chip + core)
                ref[pl.ds(row, run, stride=count * cores), :] = thrice
    two = two_ref[...]
    parts_three = parts_of(three_ref[...], rank)
    double = jnp.concatenate([parts_three, parts_three], axis=0)
    blank = jnp.zeros((parts_three.shape[0], LANES - parts_three.shape[1]), jnp.bfloat16)
    padded = jnp.concatenate([parts_three, blank], axis=1)
    empty = jnp.zeros_like(padded)
    diagonal = jnp.concatenate(
        [jnp.concatenate([padded, empty], axis=1), jnp.concatenate([empty, padded], axis=1)], axis=0
    )
    half = low_ref.shape[0]
    for row in range(half):
        lows = jnp.dot(low_ref[row], diagonal, preferred_element_type=jnp.float32)
        for each, lane in ((row, 0), (row + half, LANES)):
            through = jnp.dot(upper_ref[each], double, preferred_element_type=jnp.float32)
            through += lows[:, lane : lane + 3 * rank]
            sums_ref[each : each + 1, :] = jnp.sum(through * two, axis=0, keepdims=True)
    partial = fold_lanes(sums_ref[...], rank).T
    gram_two_ref[...] = gram_of_parts(parts_of(two, rank), rank)
    gram_three_ref[...] = gram_of_parts(parts_three, rank)
    tiles = rank // SUBLANES
    tile_two = SUBLANES * jnp.minimum(lax.axis_index("ka"), tiles - 1)
    tile_three = SUBLANES * jnp.minimum(lax.axis_index("ja"), tiles - 1)
    pieces = [partial[SUBLANES * t : SUBLANES * (t + 1)] for t in range(tiles)]
    pieces.append(gram_two_ref[pl.ds(pl.multiple_of(tile_two, SUBLANES), SUBLANES), :])
    pieces.append(gram_three_ref[pl.ds(pl.multiple_of(tile_three, SUBLANES), SUBLANES), :])
    out_ref[...] = jnp.broadcast_to(jnp.concatenate(pieces, axis=1)[None], out_ref.shape)


def across_sublanes(tile, sublane):
    return jnp.broadcast_to(tile[sublane : sublane + 1, :], tile.shape)


def across_lanes(tile, lane):
    return jnp.broadcast_to(tile[:, lane : lane + 1], tile.shape)


def eliminate(tiles, rank):
    sublane = lax.broadcasted_iota(jnp.int32, tiles[0].shape, 0)

    def reduced(values, column, pivot_row, pivot_tile, pivot_sublane):
        out = [v - c * pivot_row for v, c in zip(values, column)]
        out[pivot_tile] = jnp.where(sublane == pivot_sublane, pivot_row, out[pivot_tile])
        return out

    for begin in range(0, rank, BLOCK):
        columns = [[across_lanes(v, begin + m) for v in tiles] for m in range(BLOCK)]
        for m in range(BLOCK):
            t, s = divmod(begin + m, SUBLANES)
            column = columns[m]
            inverse = 1.0 / across_sublanes(column[t], s)
            pivot_row = across_sublanes(tiles[t], s) * inverse
            tiles = reduced(tiles, column, pivot_row, t, s)
            for later in range(m + 1, BLOCK):
                entry = across_sublanes(columns[later][t], s) * inverse
                columns[later] = reduced(columns[later], column, entry, t, s)
    return tiles


def solve_kernel(parts_ref, out_ref, updated_ref, chip_ref, *, rank, rows, cores, groups_two, groups_three, starts):
    tiles = rank // SUBLANES
    group = groups_two * groups_three
    place = {
        member: at
        for at, member in enumerate(
            itertools.product(*map(counted_from, starts, (cores, groups_two, groups_three)))
        )
    }
    products = []
    for core in range(cores):
        first = place[core, starts[1], starts[2]]
        total = parts_ref[first]
        for source in range(1, group):
            total += parts_ref[first + source]
        products.append(total)
    at_two, at_three = tiles * rows, tiles * rows + rank
    augmented = []
    for t in range(tiles):
        gram_two = parts_ref[place[0, 0, t]]
        for j in range(1, groups_two):
            gram_two += parts_ref[place[0, j, t]]
        gram_three = parts_ref[place[0, t, 0]]
        for k in range(1, groups_three):
            gram_three += parts_ref[place[0, t, k]]
        system = gram_two[:, at_two : at_two + rank] * gram_three[:, at_three : at_three + rank]
        sides = [product[:, rows * t : rows * (t + 1)] for product in products]
        augmented.append(jnp.concatenate([system] + sides, axis=1))
    solved = jnp.concatenate([v[:, rank:] for v in eliminate(augmented, rank)], axis=0)
    chip_ref[...] = solved.T
    first = pl.multiple_of(rows * lax.axis_index("core"), SUBLANES)
    updated_ref[...] = chip_ref[pl.ds(first, rows), :]
    high = solved.astype(jnp.bfloat16)
    rest = solved - high.astype(jnp.float32)
    middle = rest.astype(jnp.bfloat16)
    low = (rest - middle.astype(jnp.float32)).astype(jnp.bfloat16)
    stacked = jnp.concatenate([high, middle, low], axis=0)
    full = lax.dot_general(
        stacked, stacked, (((1,), (1,)), ((), ())), preferred_element_type=jnp.float32
    )
    gram = fold_gram(full, rank)
    pieces = [gram[SUBLANES * t : SUBLANES * (t + 1)] for t in range(tiles)]
    out_ref[...] = jnp.broadcast_to(jnp.concatenate(pieces, axis=1)[None], out_ref.shape)


def scale_kernel(grams_ref, updated_ref, factor_ref, rms_ref, correlation_ref, *, rank, total_rows):
    total = grams_ref[0]
    for source in range(1, grams_ref.shape[0]):
        total += grams_ref[source]
    gram = jnp.concatenate(
        [total[:, rank * t : rank * (t + 1)] for t in range(rank // SUBLANES)], axis=0
    )
    diagonal = jnp.where(
        lax.broadcasted_iota(jnp.int32, gram.shape, 0) == lax.broadcasted_iota(jnp.int32, gram.shape, 1),
        gram,
        0.0,
    )
    rms_row = jnp.sqrt(jnp.sum(diagonal, axis=0, keepdims=True) / total_rows + EPSILON)
    rms_column = jnp.sqrt(jnp.sum(diagonal, axis=1, keepdims=True) / total_rows + EPSILON)
    rms_ref[...] = rms_row
    factor_ref[...] = updated_ref[...] / rms_row
    correlation_ref[...] = gram / (rms_column * rms_row) / total_rows


def per_device(tensor, second_factor, third_factor):
    f32 = jnp.float32
    second_factor, third_factor = (
        pltpu.with_memory_space_constraint(v, pltpu.HBM) for v in (second_factor, third_factor)
    )
    rank = second_factor.shape[-1]
    chips, cores = lax.axis_size("z"), lax.axis_size("core")
    groups_two, groups_three = lax.axis_size("ja"), lax.axis_size("ka")
    members = chips * cores
    rows = tensor.shape[0]
    total_rows = rows * members
    slots = second_factor.shape[1] + third_factor.shape[1]
    width = -(-(lane_start(slots - 1, rank) + rank) // LANES) * LANES
    tiles = rank // SUBLANES

    packed = call(
        pack_kernel,
        jax.ShapeDtypeStruct((members, 1, width), f32),
        [
            pltpu.VMEM(second_factor.shape, f32),
            pltpu.VMEM(third_factor.shape, f32),
            pltpu.SemaphoreType.DMA((2,)),
        ],
        second_factor,
        third_factor,
        fetched=(0, 1),
    )
    rows_from = (cores - 1, chips // 2)
    plane_from = (cores - 1, groups_two // 2, groups_three // 2)
    gathered = exchange(packed, ("core", "z"), rows_from).reshape(members, width)

    upper, low = call(
        split_kernel,
        (
            jax.ShapeDtypeStruct((*tensor.shape[:2], 2 * tensor.shape[2]), jnp.bfloat16),
            jax.ShapeDtypeStruct((rows // 2, tensor.shape[1], 2 * tensor.shape[2]), jnp.bfloat16),
        ),
        [],
        tensor,
        cost=pl.CostEstimate(flops=5 * tensor.size, bytes_accessed=10 * tensor.size, transcendentals=0),
    )
    messages = call(
        functools.partial(contract_kernel, rank=rank, cores=cores, chips=chips, starts=rows_from),
        jax.ShapeDtypeStruct((cores * groups_two * groups_three, SUBLANES, tiles * rows + 2 * rank), f32),
        [
            pltpu.VMEM((tensor.shape[1], 3 * rank), f32),
            pltpu.VMEM((tensor.shape[2], 3 * rank), f32),
            pltpu.VMEM((rows, 3 * rank), f32),
            pltpu.VMEM((rank, rank), f32),
            pltpu.VMEM((rank, rank), f32),
        ],
        gathered,
        upper,
        low,
    )
    parts = exchange(messages, ("core", "ja", "ka"), plane_from)

    grams, updated = call(
        functools.partial(
            solve_kernel,
            rank=rank,
            rows=rows,
            cores=cores,
            groups_two=groups_two,
            groups_three=groups_three,
            starts=plane_from,
        ),
        (
            jax.ShapeDtypeStruct((chips, SUBLANES, tiles * rank), f32),
            jax.ShapeDtypeStruct((rows, rank), f32),
        ),
        [pltpu.VMEM((cores * rows, rank), f32)],
        parts,
    )
    grams = exchange(grams, ("z",), (chips // 2,))

    factor, column_rms, correlation = call(
        functools.partial(scale_kernel, rank=rank, total_rows=total_rows),
        (
            jax.ShapeDtypeStruct((rows, rank), f32),
            jax.ShapeDtypeStruct((1, rank), f32),
            jax.ShapeDtypeStruct((rank, rank), f32),
        ),
        [],
        grams,
        updated,
    )
    return (factor, column_rms[0], correlation)


def solution(mesh):
    ia, ja, ka = (mesh.shape[name] for name in ("ia", "ja", "ka"))
    split = Mesh(mesh.devices.reshape(ia // 2, 2, ja, ka), ("z", "core", "ja", "ka"))
    first = ("z", "core")
    return jax.shard_map(
        per_device,
        mesh=split,
        in_specs=(P(first, "ja", "ka"), P("ja", first, None), P("ka", first, None)),
        out_specs=(P(first, None), P(), P()),
        check_vma=False,
    )
```

```python
import functools
import itertools

import jax
import jax.numpy as jnp
import numpy as np
from jax import lax
from jax.experimental import pallas as pl
from jax.experimental.pallas import tpu as pltpu
from jax.sharding import Mesh, PartitionSpec as P

EPSILON = 1e-06
LANES = 128
SUBLANES = 8
BLOCK = 12
VMEM_BYTES = 8 * 2**20


def counted_from(start, size):
    return [(start + step) % size for step in range(size)]


def exchange(copies, axes, starts):
    sizes = [lax.axis_size(axis) for axis in axes]
    order = [
        int(np.ravel_multi_index(member, sizes))
        for member in itertools.product(*map(counted_from, starts, sizes))
    ]
    return lax.all_to_all(copies, axes, 0, 0, tiled=True, axis_index_groups=[order])


def lane_start(slot, rank):
    per_tile = LANES // rank
    return LANES * (slot // per_tile) + rank * (slot % per_tile)


def call(kernel, out_shape, scratch, *operands, fetched=(), cost=None):
    vmem, hbm = pl.BlockSpec(memory_space=pltpu.VMEM), pl.BlockSpec(memory_space=pltpu.HBM)
    return pl.pallas_call(
        kernel,
        out_shape=out_shape,
        in_specs=[hbm if at in fetched else vmem for at in range(len(operands))],
        out_specs=jax.tree.map(lambda _: vmem, out_shape),
        scratch_shapes=scratch,
        cost_estimate=cost,
        compiler_params=pltpu.CompilerParams(vmem_limit_bytes=VMEM_BYTES),
    )(*operands)


def pack_kernel(two_hbm, three_hbm, out_ref, two_ref, three_ref, arrived):
    copies = [
        pltpu.make_async_copy(two_hbm, two_ref, arrived.at[0]),
        pltpu.make_async_copy(three_hbm, three_ref, arrived.at[1]),
    ]
    for copy in copies:
        copy.start()
    for copy in copies:
        copy.wait()
    rank = two_ref.shape[-1]
    rows = [two_ref[0, r : r + 1, :] for r in range(two_ref.shape[1])]
    rows += [three_ref[0, r : r + 1, :] for r in range(three_ref.shape[1])]
    pieces, at = [], 0
    for slot, row in enumerate(rows):
        start = lane_start(slot, rank)
        if start > at:
            pieces.append(jnp.zeros((1, start - at), jnp.float32))
        pieces.append(row)
        at = start + rank
    pieces.append(jnp.zeros((1, out_ref.shape[-1] - at), jnp.float32))
    out_ref[...] = jnp.broadcast_to(jnp.concatenate(pieces, axis=1)[None], out_ref.shape)


def parts_of(thrice, rank):
    high = thrice.astype(jnp.bfloat16).astype(jnp.float32)
    rest = thrice - high
    middle = rest.astype(jnp.bfloat16).astype(jnp.float32)
    lane = lax.broadcasted_iota(jnp.int32, thrice.shape, 1)
    return jnp.where(
        lane < rank, high, jnp.where(lane < 2 * rank, middle, rest - middle)
    ).astype(jnp.bfloat16)


def fold_lanes(wide, rank):
    return wide[:, :rank] + wide[:, rank : 2 * rank] + wide[:, 2 * rank : 3 * rank]


def fold_gram(full, rank):
    return fold_lanes(full[:rank] + full[rank : 2 * rank] + full[2 * rank : 3 * rank], rank)


def gram_of_parts(parts, rank):
    full = lax.dot_general(
        parts, parts, (((0,), (0,)), ((), ())), preferred_element_type=jnp.float32
    )
    return fold_gram(full, rank)


def split_kernel(tensor_ref, split_ref):
    width = tensor_ref.shape[-1]

    @pl.loop(0, tensor_ref.shape[0])
    def _(row):
        cells = tensor_ref[row]
        high = cells.astype(jnp.bfloat16)
        rest = cells - high.astype(jnp.float32)
        middle = rest.astype(jnp.bfloat16)
        split_ref[row, :, :width] = high
        split_ref[row, :, width : 2 * width] = middle
        split_ref[row, :, 2 * width :] = (rest - middle.astype(jnp.float32)).astype(jnp.bfloat16)


def runs_from(start, size):
    return [(0, start, size - start)] + ([(size - start, 0, start)] if start else [])


def contract_kernel(
    gathered_ref, split_ref, out_ref, two_ref, three_ref, sums_ref,
    gram_two_ref, gram_three_ref, *, rank, cores, chips, starts
):
    count_two = two_ref.shape[0] // (cores * chips)
    count_three = three_ref.shape[0] // (cores * chips)
    for at, core in enumerate(counted_from(starts[0], cores)):
        for first, chip, run in runs_from(starts[1], chips):
            block = gathered_ref[at * chips + first : at * chips + first + run, :]
            for slot in range(count_two + count_three):
                start = lane_start(slot, rank)
                piece = block[:, start : start + rank]
                thrice = jnp.concatenate([piece, piece, piece], axis=1)
                ref, count, row = (
                    (two_ref, count_two, slot) if slot < count_two else (three_ref, count_three, slot - count_two)
                )
                row += count * (cores * chip + core)
                ref[pl.ds(row, run, stride=count * cores), :] = thrice
    two = two_ref[...]
    parts_three = parts_of(three_ref[...], rank)
    stacked = jnp.concatenate([parts_three, parts_three, parts_three], axis=0)
    for row in range(split_ref.shape[0]):
        through = jnp.dot(split_ref[row], stacked, preferred_element_type=jnp.float32)
        sums_ref[row : row + 1, :] = jnp.sum(through * two, axis=0, keepdims=True)
    partial = fold_lanes(sums_ref[...], rank).T
    gram_two_ref[...] = gram_of_parts(parts_of(two, rank), rank)
    gram_three_ref[...] = gram_of_parts(parts_three, rank)
    tiles = rank // SUBLANES
    tile_two = SUBLANES * jnp.minimum(lax.axis_index("ka"), tiles - 1)
    tile_three = SUBLANES * jnp.minimum(lax.axis_index("ja"), tiles - 1)
    pieces = [partial[SUBLANES * t : SUBLANES * (t + 1)] for t in range(tiles)]
    pieces.append(gram_two_ref[pl.ds(pl.multiple_of(tile_two, SUBLANES), SUBLANES), :])
    pieces.append(gram_three_ref[pl.ds(pl.multiple_of(tile_three, SUBLANES), SUBLANES), :])
    out_ref[...] = jnp.broadcast_to(jnp.concatenate(pieces, axis=1)[None], out_ref.shape)


def across_sublanes(tile, sublane):
    return jnp.broadcast_to(tile[sublane : sublane + 1, :], tile.shape)


def across_lanes(tile, lane):
    return jnp.broadcast_to(tile[:, lane : lane + 1], tile.shape)


def eliminate(tiles, rank):
    sublane = lax.broadcasted_iota(jnp.int32, tiles[0].shape, 0)

    def reduced(values, column, pivot_row, pivot_tile, pivot_sublane):
        out = [v - c * pivot_row for v, c in zip(values, column)]
        out[pivot_tile] = jnp.where(sublane == pivot_sublane, pivot_row, out[pivot_tile])
        return out

    for begin in range(0, rank, BLOCK):
        columns = [[across_lanes(v, begin + m) for v in tiles] for m in range(BLOCK)]
        for m in range(BLOCK):
            t, s = divmod(begin + m, SUBLANES)
            column = columns[m]
            inverse = 1.0 / across_sublanes(column[t], s)
            pivot_row = across_sublanes(tiles[t], s) * inverse
            tiles = reduced(tiles, column, pivot_row, t, s)
            for later in range(m + 1, BLOCK):
                entry = across_sublanes(columns[later][t], s) * inverse
                columns[later] = reduced(columns[later], column, entry, t, s)
    return tiles


def solve_kernel(parts_ref, out_ref, updated_ref, chip_ref, *, rank, rows, cores, groups_two, groups_three, starts):
    tiles = rank // SUBLANES
    group = groups_two * groups_three
    place = {
        member: at
        for at, member in enumerate(
            itertools.product(*map(counted_from, starts, (cores, groups_two, groups_three)))
        )
    }
    products = []
    for core in range(cores):
        first = place[core, starts[1], starts[2]]
        total = parts_ref[first]
        for source in range(1, group):
            total += parts_ref[first + source]
        products.append(total)
    at_two, at_three = tiles * rows, tiles * rows + rank
    augmented = []
    for t in range(tiles):
        gram_two = parts_ref[place[0, 0, t]]
        for j in range(1, groups_two):
            gram_two += parts_ref[place[0, j, t]]
        gram_three = parts_ref[place[0, t, 0]]
        for k in range(1, groups_three):
            gram_three += parts_ref[place[0, t, k]]
        system = gram_two[:, at_two : at_two + rank] * gram_three[:, at_three : at_three + rank]
        sides = [product[:, rows * t : rows * (t + 1)] for product in products]
        augmented.append(jnp.concatenate([system] + sides, axis=1))
    solved = jnp.concatenate([v[:, rank:] for v in eliminate(augmented, rank)], axis=0)
    chip_ref[...] = solved.T
    first = pl.multiple_of(rows * lax.axis_index("core"), SUBLANES)
    updated_ref[...] = chip_ref[pl.ds(first, rows), :]
    high = solved.astype(jnp.bfloat16)
    rest = solved - high.astype(jnp.float32)
    middle = rest.astype(jnp.bfloat16)
    low = (rest - middle.astype(jnp.float32)).astype(jnp.bfloat16)
    stacked = jnp.concatenate([high, middle, low], axis=0)
    full = lax.dot_general(
        stacked, stacked, (((1,), (1,)), ((), ())), preferred_element_type=jnp.float32
    )
    gram = fold_gram(full, rank)
    pieces = [gram[SUBLANES * t : SUBLANES * (t + 1)] for t in range(tiles)]
    out_ref[...] = jnp.broadcast_to(jnp.concatenate(pieces, axis=1)[None], out_ref.shape)


def scale_kernel(grams_ref, updated_ref, factor_ref, rms_ref, correlation_ref, *, rank, total_rows):
    total = grams_ref[0]
    for source in range(1, grams_ref.shape[0]):
        total += grams_ref[source]
    gram = jnp.concatenate(
        [total[:, rank * t : rank * (t + 1)] for t in range(rank // SUBLANES)], axis=0
    )
    diagonal = jnp.where(
        lax.broadcasted_iota(jnp.int32, gram.shape, 0) == lax.broadcasted_iota(jnp.int32, gram.shape, 1),
        gram,
        0.0,
    )
    rms_row = jnp.sqrt(jnp.sum(diagonal, axis=0, keepdims=True) / total_rows + EPSILON)
    rms_column = jnp.sqrt(jnp.sum(diagonal, axis=1, keepdims=True) / total_rows + EPSILON)
    rms_ref[...] = rms_row
    factor_ref[...] = updated_ref[...] / rms_row
    correlation_ref[...] = gram / (rms_column * rms_row) / total_rows


def per_device(tensor, second_factor, third_factor):
    f32 = jnp.float32
    second_factor, third_factor = (
        pltpu.with_memory_space_constraint(v, pltpu.HBM) for v in (second_factor, third_factor)
    )
    rank = second_factor.shape[-1]
    chips, cores = lax.axis_size("z"), lax.axis_size("core")
    groups_two, groups_three = lax.axis_size("ja"), lax.axis_size("ka")
    members = chips * cores
    rows = tensor.shape[0]
    total_rows = rows * members
    slots = second_factor.shape[1] + third_factor.shape[1]
    width = -(-(lane_start(slots - 1, rank) + rank) // LANES) * LANES
    tiles = rank // SUBLANES

    packed = call(
        pack_kernel,
        jax.ShapeDtypeStruct((members, 1, width), f32),
        [
            pltpu.VMEM(second_factor.shape, f32),
            pltpu.VMEM(third_factor.shape, f32),
            pltpu.SemaphoreType.DMA((2,)),
        ],
        second_factor,
        third_factor,
        fetched=(0, 1),
    )
    rows_from = (cores - 1, 5 * chips // 8)
    plane_from = (cores - 1, groups_two // 2, groups_three // 2)
    gathered = exchange(packed, ("core", "z"), rows_from).reshape(members, width)

    split = call(
        split_kernel,
        jax.ShapeDtypeStruct((*tensor.shape[:2], 3 * tensor.shape[2]), jnp.bfloat16),
        [],
        tensor,
        cost=pl.CostEstimate(flops=5 * tensor.size, bytes_accessed=10 * tensor.size, transcendentals=0),
    )
    messages = call(
        functools.partial(contract_kernel, rank=rank, cores=cores, chips=chips, starts=rows_from),
        jax.ShapeDtypeStruct((cores * groups_two * groups_three, SUBLANES, tiles * rows + 2 * rank), f32),
        [
            pltpu.VMEM((tensor.shape[1], 3 * rank), f32),
            pltpu.VMEM((tensor.shape[2], 3 * rank), f32),
            pltpu.VMEM((rows, 3 * rank), f32),
            pltpu.VMEM((rank, rank), f32),
            pltpu.VMEM((rank, rank), f32),
        ],
        gathered,
        split,
    )
    parts = exchange(messages, ("core", "ja", "ka"), plane_from)

    grams, updated = call(
        functools.partial(
            solve_kernel,
            rank=rank,
            rows=rows,
            cores=cores,
            groups_two=groups_two,
            groups_three=groups_three,
            starts=plane_from,
        ),
        (
            jax.ShapeDtypeStruct((chips, SUBLANES, tiles * rank), f32),
            jax.ShapeDtypeStruct((rows, rank), f32),
        ),
        [pltpu.VMEM((cores * rows, rank), f32)],
        parts,
    )
    grams = exchange(grams, ("z",), (chips // 2 + 1,))

    factor, column_rms, correlation = call(
        functools.partial(scale_kernel, rank=rank, total_rows=total_rows),
        (
            jax.ShapeDtypeStruct((rows, rank), f32),
            jax.ShapeDtypeStruct((1, rank), f32),
            jax.ShapeDtypeStruct((rank, rank), f32),
        ),
        [],
        grams,
        updated,
    )
    return (factor, column_rms[0], correlation)


def solution(mesh):
    ia, ja, ka = (mesh.shape[name] for name in ("ia", "ja", "ka"))
    split = Mesh(mesh.devices.reshape(ia // 2, 2, ja, ka), ("z", "core", "ja", "ka"))
    first = ("z", "core")
    return jax.shard_map(
        per_device,
        mesh=split,
        in_specs=(P(first, "ja", "ka"), P("ja", first, None), P("ka", first, None)),
        out_specs=(P(first, None), P(), P()),
        check_vma=False,
    )
```

```python
import functools
import itertools

import jax
import jax.numpy as jnp
import numpy as np
from jax import lax
from jax.experimental import pallas as pl
from jax.experimental.pallas import tpu as pltpu
from jax.sharding import Mesh, PartitionSpec as P

EPSILON = 1e-06
LANES = 128
SUBLANES = 8
QUAD = 4
BLOCK = 12
VMEM_BYTES = 8 * 2**20


def counted_from(start, size):
    return [(start + step) % size for step in range(size)]


def exchange(copies, axes, starts):
    sizes = [lax.axis_size(axis) for axis in axes]
    order = [
        int(np.ravel_multi_index(member, sizes))
        for member in itertools.product(*map(counted_from, starts, sizes))
    ]
    return lax.all_to_all(copies, axes, 0, 0, tiled=True, axis_index_groups=[order])


def lane_start(slot, rank):
    per_tile = LANES // rank
    return LANES * (slot // per_tile) + rank * (slot % per_tile)


def call(kernel, out_shape, scratch, *operands, fetched=(), cost=None):
    vmem, hbm = pl.BlockSpec(memory_space=pltpu.VMEM), pl.BlockSpec(memory_space=pltpu.HBM)
    return pl.pallas_call(
        kernel,
        out_shape=out_shape,
        in_specs=[hbm if at in fetched else vmem for at in range(len(operands))],
        out_specs=jax.tree.map(lambda _: vmem, out_shape),
        scratch_shapes=scratch,
        cost_estimate=cost,
        compiler_params=pltpu.CompilerParams(vmem_limit_bytes=VMEM_BYTES),
    )(*operands)


def pack_kernel(two_hbm, three_hbm, out_ref, two_ref, three_ref, arrived):
    copies = [
        pltpu.make_async_copy(two_hbm, two_ref, arrived.at[0]),
        pltpu.make_async_copy(three_hbm, three_ref, arrived.at[1]),
    ]
    for copy in copies:
        copy.start()
    for copy in copies:
        copy.wait()
    rank = two_ref.shape[-1]
    rows = [two_ref[0, r : r + 1, :] for r in range(two_ref.shape[1])]
    rows += [three_ref[0, r : r + 1, :] for r in range(three_ref.shape[1])]
    pieces, at = [], 0
    for slot, row in enumerate(rows):
        start = lane_start(slot, rank)
        if start > at:
            pieces.append(jnp.zeros((1, start - at), jnp.float32))
        pieces.append(row)
        at = start + rank
    pieces.append(jnp.zeros((1, out_ref.shape[-1] - at), jnp.float32))
    out_ref[...] = jnp.broadcast_to(jnp.concatenate(pieces, axis=1)[None], out_ref.shape)


def parts_of(thrice, rank):
    high = thrice.astype(jnp.bfloat16).astype(jnp.float32)
    rest = thrice - high
    middle = rest.astype(jnp.bfloat16).astype(jnp.float32)
    lane = lax.broadcasted_iota(jnp.int32, thrice.shape, 1)
    return jnp.where(
        lane < rank, high, jnp.where(lane < 2 * rank, middle, rest - middle)
    ).astype(jnp.bfloat16)


def fold_lanes(wide, rank):
    return wide[:, :rank] + wide[:, rank : 2 * rank] + wide[:, 2 * rank : 3 * rank]


def fold_gram(full, rank):
    return fold_lanes(full[:rank] + full[rank : 2 * rank] + full[2 * rank : 3 * rank], rank)


def gram_of_parts(parts, rank):
    full = lax.dot_general(
        parts, parts, (((0,), (0,)), ((), ())), preferred_element_type=jnp.float32
    )
    return fold_gram(full, rank)


def split_kernel(tensor_ref, split_ref):
    width = tensor_ref.shape[-1]

    @pl.loop(0, tensor_ref.shape[0])
    def _(row):
        cells = tensor_ref[row]
        high = cells.astype(jnp.bfloat16)
        rest = cells - high.astype(jnp.float32)
        middle = rest.astype(jnp.bfloat16)
        split_ref[row, :, :width] = high
        split_ref[row, :, width : 2 * width] = middle
        split_ref[row, :, 2 * width :] = (rest - middle.astype(jnp.float32)).astype(jnp.bfloat16)


def runs_from(start, size):
    return [(0, start, size - start)] + ([(size - start, 0, start)] if start else [])


def contract_kernel(
    gathered_ref, split_ref, out_ref, two_ref, three_ref, sums_ref,
    gram_two_ref, gram_three_ref, *, rank, cores, chips, starts
):
    count_two = two_ref.shape[0] // (cores * chips)
    count_three = three_ref.shape[0] // (cores * chips)
    for at, core in enumerate(counted_from(starts[0], cores)):
        for first, chip, run in runs_from(starts[1], chips):
            block = gathered_ref[at * chips + first : at * chips + first + run, :]
            for slot in range(count_two + count_three):
                start = lane_start(slot, rank)
                piece = block[:, start : start + rank]
                thrice = jnp.concatenate([piece, piece, piece], axis=1)
                ref, count, row = (
                    (two_ref, count_two, slot) if slot < count_two else (three_ref, count_three, slot - count_two)
                )
                row += count * (cores * chip + core)
                ref[pl.ds(row, run, stride=count * cores), :] = thrice
    two = two_ref[...]
    parts_three = parts_of(three_ref[...], rank)
    stacked = jnp.concatenate([parts_three, parts_three, parts_three], axis=0)
    for row in range(split_ref.shape[0]):
        through = jnp.dot(split_ref[row], stacked, preferred_element_type=jnp.float32)
        sums_ref[row : row + 1, :] = jnp.sum(through * two, axis=0, keepdims=True)
    partial = fold_lanes(sums_ref[...], rank).T
    gram_two_ref[...] = gram_of_parts(parts_of(two, rank), rank)
    gram_three_ref[...] = gram_of_parts(parts_three, rank)
    tiles = rank // SUBLANES
    tile_two = SUBLANES * jnp.minimum(lax.axis_index("ka"), tiles - 1)
    tile_three = SUBLANES * jnp.minimum(lax.axis_index("ja"), tiles - 1)
    pieces = [partial[SUBLANES * t : SUBLANES * (t + 1)] for t in range(tiles)]
    pieces.append(gram_two_ref[pl.ds(pl.multiple_of(tile_two, SUBLANES), SUBLANES), :])
    pieces.append(gram_three_ref[pl.ds(pl.multiple_of(tile_three, SUBLANES), SUBLANES), :])
    out_ref[...] = jnp.broadcast_to(jnp.concatenate(pieces, axis=1)[None], out_ref.shape)


def upper_spans(rank):
    return [(first, sum(rank - f for f in range(0, first, QUAD))) for first in range(0, rank, QUAD)]


def upper_width(rank):
    return sum(rank - first for first in range(0, rank, QUAD))


def upper_rows(full):
    rank = full.shape[0]
    return jnp.concatenate([full[f : f + QUAD, f:] for f, _ in upper_spans(rank)], axis=1)


def from_upper_rows(packed, rank):
    rows = []
    for first, at in upper_spans(rank):
        piece = packed[:, at : at + rank - first]
        rows.append(jnp.concatenate([jnp.zeros((QUAD, first), jnp.float32), piece], axis=1) if first else piece)
    upper = jnp.concatenate(rows, axis=0)
    down = lax.broadcasted_iota(jnp.int32, upper.shape, 0) // QUAD
    right = lax.broadcasted_iota(jnp.int32, upper.shape, 1) // QUAD
    return jnp.where(down > right, upper.T, upper)


def across_sublanes(tile, sublane):
    return jnp.broadcast_to(tile[sublane : sublane + 1, :], tile.shape)


def across_lanes(tile, lane):
    return jnp.broadcast_to(tile[:, lane : lane + 1], tile.shape)


def eliminate(tiles, rank):
    sublane = lax.broadcasted_iota(jnp.int32, tiles[0].shape, 0)

    def reduced(values, column, pivot_row, pivot_tile, pivot_sublane):
        out = [v - c * pivot_row for v, c in zip(values, column)]
        out[pivot_tile] = jnp.where(sublane == pivot_sublane, pivot_row, out[pivot_tile])
        return out

    for begin in range(0, rank, BLOCK):
        columns = [[across_lanes(v, begin + m) for v in tiles] for m in range(BLOCK)]
        for m in range(BLOCK):
            t, s = divmod(begin + m, SUBLANES)
            column = columns[m]
            inverse = 1.0 / across_sublanes(column[t], s)
            pivot_row = across_sublanes(tiles[t], s) * inverse
            tiles = reduced(tiles, column, pivot_row, t, s)
            for later in range(m + 1, BLOCK):
                entry = across_sublanes(columns[later][t], s) * inverse
                columns[later] = reduced(columns[later], column, entry, t, s)
    return tiles


def solve_kernel(parts_ref, out_ref, updated_ref, chip_ref, *, rank, rows, cores, groups_two, groups_three, starts):
    tiles = rank // SUBLANES
    group = groups_two * groups_three
    place = {
        member: at
        for at, member in enumerate(
            itertools.product(*map(counted_from, starts, (cores, groups_two, groups_three)))
        )
    }
    products = []
    for core in range(cores):
        first = place[core, starts[1], starts[2]]
        total = parts_ref[first]
        for source in range(1, group):
            total += parts_ref[first + source]
        products.append(total)
    at_two, at_three = tiles * rows, tiles * rows + rank
    augmented = []
    for t in range(tiles):
        gram_two = parts_ref[place[0, 0, t]]
        for j in range(1, groups_two):
            gram_two += parts_ref[place[0, j, t]]
        gram_three = parts_ref[place[0, t, 0]]
        for k in range(1, groups_three):
            gram_three += parts_ref[place[0, t, k]]
        system = gram_two[:, at_two : at_two + rank] * gram_three[:, at_three : at_three + rank]
        sides = [product[:, rows * t : rows * (t + 1)] for product in products]
        augmented.append(jnp.concatenate([system] + sides, axis=1))
    solved = jnp.concatenate([v[:, rank:] for v in eliminate(augmented, rank)], axis=0)
    chip_ref[...] = solved.T
    first = pl.multiple_of(rows * lax.axis_index("core"), SUBLANES)
    updated_ref[...] = chip_ref[pl.ds(first, rows), :]
    high = solved.astype(jnp.bfloat16)
    rest = solved - high.astype(jnp.float32)
    middle = rest.astype(jnp.bfloat16)
    low = (rest - middle.astype(jnp.float32)).astype(jnp.bfloat16)
    stacked = jnp.concatenate([high, middle, low], axis=0)
    full = lax.dot_general(
        stacked, stacked, (((1,), (1,)), ((), ())), preferred_element_type=jnp.float32
    )
    gram = fold_gram(full, rank)
    out_ref[...] = jnp.broadcast_to(upper_rows(gram)[None], out_ref.shape)


def scale_kernel(grams_ref, updated_ref, factor_ref, rms_ref, correlation_ref, *, rank, total_rows):
    total = grams_ref[0]
    for source in range(1, grams_ref.shape[0]):
        total += grams_ref[source]
    gram = from_upper_rows(total, rank)
    diagonal = jnp.where(
        lax.broadcasted_iota(jnp.int32, gram.shape, 0) == lax.broadcasted_iota(jnp.int32, gram.shape, 1),
        gram,
        0.0,
    )
    rms_row = jnp.sqrt(jnp.sum(diagonal, axis=0, keepdims=True) / total_rows + EPSILON)
    rms_column = jnp.sqrt(jnp.sum(diagonal, axis=1, keepdims=True) / total_rows + EPSILON)
    rms_ref[...] = rms_row
    factor_ref[...] = updated_ref[...] / rms_row
    correlation_ref[...] = gram / (rms_column * rms_row) / total_rows


def per_device(tensor, second_factor, third_factor):
    f32 = jnp.float32
    second_factor, third_factor = (
        pltpu.with_memory_space_constraint(v, pltpu.HBM) for v in (second_factor, third_factor)
    )
    rank = second_factor.shape[-1]
    chips, cores = lax.axis_size("z"), lax.axis_size("core")
    groups_two, groups_three = lax.axis_size("ja"), lax.axis_size("ka")
    members = chips * cores
    rows = tensor.shape[0]
    total_rows = rows * members
    slots = second_factor.shape[1] + third_factor.shape[1]
    width = -(-(lane_start(slots - 1, rank) + rank) // LANES) * LANES
    tiles = rank // SUBLANES

    packed = call(
        pack_kernel,
        jax.ShapeDtypeStruct((members, 1, width), f32),
        [
            pltpu.VMEM(second_factor.shape, f32),
            pltpu.VMEM(third_factor.shape, f32),
            pltpu.SemaphoreType.DMA((2,)),
        ],
        second_factor,
        third_factor,
        fetched=(0, 1),
    )
    rows_from = (cores - 1, 5 * chips // 8)
    plane_from = (cores - 1, groups_two // 2, groups_three // 2)
    gathered = exchange(packed, ("core", "z"), rows_from).reshape(members, width)

    split = call(
        split_kernel,
        jax.ShapeDtypeStruct((*tensor.shape[:2], 3 * tensor.shape[2]), jnp.bfloat16),
        [],
        tensor,
        cost=pl.CostEstimate(flops=5 * tensor.size, bytes_accessed=10 * tensor.size, transcendentals=0),
    )
    messages = call(
        functools.partial(contract_kernel, rank=rank, cores=cores, chips=chips, starts=rows_from),
        jax.ShapeDtypeStruct((cores * groups_two * groups_three, SUBLANES, tiles * rows + 2 * rank), f32),
        [
            pltpu.VMEM((tensor.shape[1], 3 * rank), f32),
            pltpu.VMEM((tensor.shape[2], 3 * rank), f32),
            pltpu.VMEM((rows, 3 * rank), f32),
            pltpu.VMEM((rank, rank), f32),
            pltpu.VMEM((rank, rank), f32),
        ],
        gathered,
        split,
    )
    parts = exchange(messages, ("core", "ja", "ka"), plane_from)

    grams, updated = call(
        functools.partial(
            solve_kernel,
            rank=rank,
            rows=rows,
            cores=cores,
            groups_two=groups_two,
            groups_three=groups_three,
            starts=plane_from,
        ),
        (
            jax.ShapeDtypeStruct((chips, QUAD, upper_width(rank)), f32),
            jax.ShapeDtypeStruct((rows, rank), f32),
        ),
        [pltpu.VMEM((cores * rows, rank), f32)],
        parts,
    )
    grams = exchange(grams, ("z",), (chips // 2 + 1,))

    factor, column_rms, correlation = call(
        functools.partial(scale_kernel, rank=rank, total_rows=total_rows),
        (
            jax.ShapeDtypeStruct((rows, rank), f32),
            jax.ShapeDtypeStruct((1, rank), f32),
            jax.ShapeDtypeStruct((rank, rank), f32),
        ),
        [],
        grams,
        updated,
    )
    return (factor, column_rms[0], correlation)


def solution(mesh):
    ia, ja, ka = (mesh.shape[name] for name in ("ia", "ja", "ka"))
    split = Mesh(mesh.devices.reshape(ia // 2, 2, ja, ka), ("z", "core", "ja", "ka"))
    first = ("z", "core")
    return jax.shard_map(
        per_device,
        mesh=split,
        in_specs=(P(first, "ja", "ka"), P("ja", first, None), P("ka", first, None)),
        out_specs=(P(first, None), P(), P()),
        check_vma=False,
    )
```

```python
import functools
import itertools

import jax
import jax.numpy as jnp
import numpy as np
from jax import lax
from jax.experimental import pallas as pl
from jax.experimental.pallas import tpu as pltpu
from jax.sharding import Mesh, PartitionSpec as P

EPSILON = 1e-06
LANES = 128
SUBLANES = 8
QUAD = 4
BLOCK = 12
VMEM_BYTES = 8 * 2**20


def counted_from(start, size):
    return [(start + step) % size for step in range(size)]


def upper_first(start, size):
    half = size // 2
    return [half + at for at in counted_from(start - half, half)] + list(range(half))


def exchange(copies, axes, orders):
    sizes = [lax.axis_size(axis) for axis in axes]
    listed = [int(np.ravel_multi_index(member, sizes)) for member in itertools.product(*orders)]
    return lax.all_to_all(copies, axes, 0, 0, tiled=True, axis_index_groups=[listed])


def lane_start(slot, rank):
    per_tile = LANES // rank
    return LANES * (slot // per_tile) + rank * (slot % per_tile)


def call(kernel, out_shape, scratch, *operands, fetched=(), cost=None):
    vmem, hbm = pl.BlockSpec(memory_space=pltpu.VMEM), pl.BlockSpec(memory_space=pltpu.HBM)
    return pl.pallas_call(
        kernel,
        out_shape=out_shape,
        in_specs=[hbm if at in fetched else vmem for at in range(len(operands))],
        out_specs=jax.tree.map(lambda _: vmem, out_shape),
        scratch_shapes=scratch,
        cost_estimate=cost,
        compiler_params=pltpu.CompilerParams(vmem_limit_bytes=VMEM_BYTES),
    )(*operands)


def pack_kernel(two_hbm, three_hbm, out_ref, two_ref, three_ref, arrived):
    copies = [
        pltpu.make_async_copy(two_hbm, two_ref, arrived.at[0]),
        pltpu.make_async_copy(three_hbm, three_ref, arrived.at[1]),
    ]
    for copy in copies:
        copy.start()
    for copy in copies:
        copy.wait()
    rank = two_ref.shape[-1]
    rows = [two_ref[0, r : r + 1, :] for r in range(two_ref.shape[1])]
    rows += [three_ref[0, r : r + 1, :] for r in range(three_ref.shape[1])]
    pieces, at = [], 0
    for slot, row in enumerate(rows):
        start = lane_start(slot, rank)
        if start > at:
            pieces.append(jnp.zeros((1, start - at), jnp.float32))
        pieces.append(row)
        at = start + rank
    pieces.append(jnp.zeros((1, out_ref.shape[-1] - at), jnp.float32))
    out_ref[...] = jnp.broadcast_to(jnp.concatenate(pieces, axis=1)[None], out_ref.shape)


def parts_of(thrice, rank):
    high = thrice.astype(jnp.bfloat16).astype(jnp.float32)
    rest = thrice - high
    middle = rest.astype(jnp.bfloat16).astype(jnp.float32)
    lane = lax.broadcasted_iota(jnp.int32, thrice.shape, 1)
    return jnp.where(
        lane < rank, high, jnp.where(lane < 2 * rank, middle, rest - middle)
    ).astype(jnp.bfloat16)


def fold_lanes(wide, rank):
    return wide[:, :rank] + wide[:, rank : 2 * rank] + wide[:, 2 * rank : 3 * rank]


def fold_gram(full, rank):
    return fold_lanes(full[:rank] + full[rank : 2 * rank] + full[2 * rank : 3 * rank], rank)


def gram_of_parts(parts, rank):
    full = lax.dot_general(
        parts, parts, (((0,), (0,)), ((), ())), preferred_element_type=jnp.float32
    )
    return fold_gram(full, rank)


def split_kernel(tensor_ref, split_ref):
    width = tensor_ref.shape[-1]

    @pl.loop(0, tensor_ref.shape[0])
    def _(row):
        cells = tensor_ref[row]
        high = cells.astype(jnp.bfloat16)
        rest = cells - high.astype(jnp.float32)
        middle = rest.astype(jnp.bfloat16)
        split_ref[row, :, :width] = high
        split_ref[row, :, width : 2 * width] = middle
        split_ref[row, :, 2 * width :] = (rest - middle.astype(jnp.float32)).astype(jnp.bfloat16)


def contract_kernel(
    gathered_ref, split_ref, out_ref, two_ref, three_ref, sums_ref,
    gram_two_ref, gram_three_ref, *, rank, orders
):
    cores, chips = map(len, orders)
    count_two = two_ref.shape[0] // (cores * chips)
    count_three = three_ref.shape[0] // (cores * chips)
    half = chips // 2
    for at, core in enumerate(orders[0]):
        for first in range(0, chips, half):
            block = gathered_ref[at * chips + first : at * chips + first + half, :]
            chip = min(orders[1][first : first + half])
            turn = orders[1].index(chip) - first
            if turn:
                block = jnp.concatenate([block[turn:], block[:turn]], axis=0)
            for slot in range(count_two + count_three):
                start = lane_start(slot, rank)
                piece = block[:, start : start + rank]
                thrice = jnp.concatenate([piece, piece, piece], axis=1)
                ref, count, row = (
                    (two_ref, count_two, slot) if slot < count_two else (three_ref, count_three, slot - count_two)
                )
                row += count * (cores * chip + core)
                ref[pl.ds(row, half, stride=count * cores), :] = thrice
    two = two_ref[...]
    parts_three = parts_of(three_ref[...], rank)
    stacked = jnp.concatenate([parts_three, parts_three, parts_three], axis=0)
    for row in range(split_ref.shape[0]):
        through = jnp.dot(split_ref[row], stacked, preferred_element_type=jnp.float32)
        sums_ref[row : row + 1, :] = jnp.sum(through * two, axis=0, keepdims=True)
    partial = fold_lanes(sums_ref[...], rank).T
    gram_two_ref[...] = gram_of_parts(parts_of(two, rank), rank)
    gram_three_ref[...] = gram_of_parts(parts_three, rank)
    tiles = rank // SUBLANES
    tile_two = SUBLANES * jnp.minimum(lax.axis_index("ka"), tiles - 1)
    tile_three = SUBLANES * jnp.minimum(lax.axis_index("ja"), tiles - 1)
    pieces = [partial[SUBLANES * t : SUBLANES * (t + 1)] for t in range(tiles)]
    pieces.append(gram_two_ref[pl.ds(pl.multiple_of(tile_two, SUBLANES), SUBLANES), :])
    pieces.append(gram_three_ref[pl.ds(pl.multiple_of(tile_three, SUBLANES), SUBLANES), :])
    out_ref[...] = jnp.broadcast_to(jnp.concatenate(pieces, axis=1)[None], out_ref.shape)


def upper_spans(rank):
    return [(first, sum(rank - f for f in range(0, first, QUAD))) for first in range(0, rank, QUAD)]


def upper_width(rank):
    return sum(rank - first for first in range(0, rank, QUAD))


def upper_rows(full):
    rank = full.shape[0]
    return jnp.concatenate([full[f : f + QUAD, f:] for f, _ in upper_spans(rank)], axis=1)


def from_upper_rows(packed, rank):
    rows = []
    for first, at in upper_spans(rank):
        piece = packed[:, at : at + rank - first]
        rows.append(jnp.concatenate([jnp.zeros((QUAD, first), jnp.float32), piece], axis=1) if first else piece)
    upper = jnp.concatenate(rows, axis=0)
    down = lax.broadcasted_iota(jnp.int32, upper.shape, 0) // QUAD
    right = lax.broadcasted_iota(jnp.int32, upper.shape, 1) // QUAD
    return jnp.where(down > right, upper.T, upper)


def across_sublanes(tile, sublane):
    return jnp.broadcast_to(tile[sublane : sublane + 1, :], tile.shape)


def across_lanes(tile, lane):
    return jnp.broadcast_to(tile[:, lane : lane + 1], tile.shape)


def eliminate(tiles, rank):
    sublane = lax.broadcasted_iota(jnp.int32, tiles[0].shape, 0)

    def reduced(values, column, pivot_row, pivot_tile, pivot_sublane):
        out = [v - c * pivot_row for v, c in zip(values, column)]
        out[pivot_tile] = jnp.where(sublane == pivot_sublane, pivot_row, out[pivot_tile])
        return out

    for begin in range(0, rank, BLOCK):
        columns = [[across_lanes(v, begin + m) for v in tiles] for m in range(BLOCK)]
        pivot = across_sublanes(columns[0][begin // SUBLANES], begin % SUBLANES)
        for m in range(BLOCK):
            t, s = divmod(begin + m, SUBLANES)
            column = columns[m]
            inverse = 1.0 / pivot
            pivot_row = across_sublanes(tiles[t], s) * inverse
            if m + 1 < BLOCK:
                after = columns[m + 1]
                entry = across_sublanes(after[t], s) * inverse
                t_after, s_after = divmod(begin + m + 1, SUBLANES)
                pivot = across_sublanes(after[t_after], s_after)
                pivot -= across_sublanes(column[t_after], s_after) * entry
            tiles = reduced(tiles, column, pivot_row, t, s)
            for later in range(m + 1, BLOCK):
                entry = across_sublanes(columns[later][t], s) * inverse
                columns[later] = reduced(columns[later], column, entry, t, s)
    return tiles


def solve_kernel(parts_ref, out_ref, updated_ref, chip_ref, *, rank, rows, orders):
    tiles = rank // SUBLANES
    cores, groups_two, groups_three = map(len, orders)
    group = groups_two * groups_three
    place = {member: at for at, member in enumerate(itertools.product(*orders))}
    products = []
    for core in range(cores):
        first = place[core, orders[1][0], orders[2][0]]
        total = parts_ref[first]
        for source in range(1, group):
            total += parts_ref[first + source]
        products.append(total)
    at_two, at_three = tiles * rows, tiles * rows + rank
    augmented = []
    for t in range(tiles):
        gram_two = parts_ref[place[0, 0, t]]
        for j in range(1, groups_two):
            gram_two += parts_ref[place[0, j, t]]
        gram_three = parts_ref[place[0, t, 0]]
        for k in range(1, groups_three):
            gram_three += parts_ref[place[0, t, k]]
        system = gram_two[:, at_two : at_two + rank] * gram_three[:, at_three : at_three + rank]
        sides = [product[:, rows * t : rows * (t + 1)] for product in products]
        augmented.append(jnp.concatenate([system] + sides, axis=1))
    solved = jnp.concatenate([v[:, rank:] for v in eliminate(augmented, rank)], axis=0)
    chip_ref[...] = solved.T
    first = pl.multiple_of(rows * lax.axis_index("core"), SUBLANES)
    updated_ref[...] = chip_ref[pl.ds(first, rows), :]
    high = solved.astype(jnp.bfloat16)
    rest = solved - high.astype(jnp.float32)
    middle = rest.astype(jnp.bfloat16)
    low = (rest - middle.astype(jnp.float32)).astype(jnp.bfloat16)
    stacked = jnp.concatenate([high, middle, low], axis=0)
    full = lax.dot_general(
        stacked, stacked, (((1,), (1,)), ((), ())), preferred_element_type=jnp.float32
    )
    gram = fold_gram(full, rank)
    out_ref[...] = jnp.broadcast_to(upper_rows(gram)[None], out_ref.shape)


def scale_kernel(grams_ref, updated_ref, factor_ref, rms_ref, correlation_ref, *, rank, total_rows):
    total = grams_ref[0]
    for source in range(1, grams_ref.shape[0]):
        total += grams_ref[source]
    gram = from_upper_rows(total, rank)
    diagonal = jnp.where(
        lax.broadcasted_iota(jnp.int32, gram.shape, 0) == lax.broadcasted_iota(jnp.int32, gram.shape, 1),
        gram,
        0.0,
    )
    rms_row = jnp.sqrt(jnp.sum(diagonal, axis=0, keepdims=True) / total_rows + EPSILON)
    rms_column = jnp.sqrt(jnp.sum(diagonal, axis=1, keepdims=True) / total_rows + EPSILON)
    rms_ref[...] = rms_row
    factor_ref[...] = updated_ref[...] / rms_row
    correlation_ref[...] = gram / (rms_column * rms_row) / total_rows


def per_device(tensor, second_factor, third_factor):
    f32 = jnp.float32
    second_factor, third_factor = (
        pltpu.with_memory_space_constraint(v, pltpu.HBM) for v in (second_factor, third_factor)
    )
    rank = second_factor.shape[-1]
    chips, cores = lax.axis_size("z"), lax.axis_size("core")
    groups_two, groups_three = lax.axis_size("ja"), lax.axis_size("ka")
    members = chips * cores
    rows = tensor.shape[0]
    total_rows = rows * members
    slots = second_factor.shape[1] + third_factor.shape[1]
    width = -(-(lane_start(slots - 1, rank) + rank) // LANES) * LANES
    tiles = rank // SUBLANES

    packed = call(
        pack_kernel,
        jax.ShapeDtypeStruct((members, 1, width), f32),
        [
            pltpu.VMEM(second_factor.shape, f32),
            pltpu.VMEM(third_factor.shape, f32),
            pltpu.SemaphoreType.DMA((2,)),
        ],
        second_factor,
        third_factor,
        fetched=(0, 1),
    )
    cores_order = counted_from(cores - 1, cores)
    rows_order = (cores_order, upper_first(5 * chips // 8, chips))
    plane_order = (
        cores_order,
        counted_from(groups_two // 2, groups_two),
        counted_from(groups_three // 2, groups_three),
    )
    chips_order = (counted_from(chips // 2 + 1, chips),)
    gathered = exchange(packed, ("core", "z"), rows_order).reshape(members, width)

    split = call(
        split_kernel,
        jax.ShapeDtypeStruct((*tensor.shape[:2], 3 * tensor.shape[2]), jnp.bfloat16),
        [],
        tensor,
        cost=pl.CostEstimate(flops=5 * tensor.size, bytes_accessed=10 * tensor.size, transcendentals=0),
    )
    messages = call(
        functools.partial(contract_kernel, rank=rank, orders=rows_order),
        jax.ShapeDtypeStruct((cores * groups_two * groups_three, SUBLANES, tiles * rows + 2 * rank), f32),
        [
            pltpu.VMEM((tensor.shape[1], 3 * rank), f32),
            pltpu.VMEM((tensor.shape[2], 3 * rank), f32),
            pltpu.VMEM((rows, 3 * rank), f32),
            pltpu.VMEM((rank, rank), f32),
            pltpu.VMEM((rank, rank), f32),
        ],
        gathered,
        split,
    )
    parts = exchange(messages, ("core", "ja", "ka"), plane_order)

    grams, updated = call(
        functools.partial(solve_kernel, rank=rank, rows=rows, orders=plane_order),
        (
            jax.ShapeDtypeStruct((chips, QUAD, upper_width(rank)), f32),
            jax.ShapeDtypeStruct((rows, rank), f32),
        ),
        [pltpu.VMEM((cores * rows, rank), f32)],
        parts,
    )
    grams = exchange(grams, ("z",), chips_order)

    factor, column_rms, correlation = call(
        functools.partial(scale_kernel, rank=rank, total_rows=total_rows),
        (
            jax.ShapeDtypeStruct((rows, rank), f32),
            jax.ShapeDtypeStruct((1, rank), f32),
            jax.ShapeDtypeStruct((rank, rank), f32),
        ),
        [],
        grams,
        updated,
    )
    return (factor, column_rms[0], correlation)


def solution(mesh):
    ia, ja, ka = (mesh.shape[name] for name in ("ia", "ja", "ka"))
    split = Mesh(mesh.devices.reshape(ia // 2, 2, ja, ka), ("z", "core", "ja", "ka"))
    first = ("z", "core")
    return jax.shard_map(
        per_device,
        mesh=split,
        in_specs=(P(first, "ja", "ka"), P("ja", first, None), P("ka", first, None)),
        out_specs=(P(first, None), P(), P()),
        check_vma=False,
    )
```

```python
import functools
import itertools

import jax
import jax.numpy as jnp
import numpy as np
from jax import lax
from jax.experimental import pallas as pl
from jax.experimental.pallas import tpu as pltpu
from jax.sharding import Mesh, PartitionSpec as P

EPSILON = 1e-06
LANES = 128
SUBLANES = 8
QUAD = 4
BLOCK = 12
VMEM_BYTES = 8 * 2**20


def counted_from(start, size):
    return [(start + step) % size for step in range(size)]


def upper_first(start, size):
    half = size // 2
    return [half + at for at in counted_from(start - half, half)] + list(range(half))


def exchange(copies, axes, orders):
    sizes = [lax.axis_size(axis) for axis in axes]
    listed = [int(np.ravel_multi_index(member, sizes)) for member in itertools.product(*orders)]
    return lax.all_to_all(copies, axes, 0, 0, tiled=True, axis_index_groups=[listed])


def lane_start(slot, rank):
    per_tile = LANES // rank
    return LANES * (slot // per_tile) + rank * (slot % per_tile)


def call(kernel, out_shape, scratch, *operands, fetched=(), cost=None):
    vmem, hbm = pl.BlockSpec(memory_space=pltpu.VMEM), pl.BlockSpec(memory_space=pltpu.HBM)
    return pl.pallas_call(
        kernel,
        out_shape=out_shape,
        in_specs=[hbm if at in fetched else vmem for at in range(len(operands))],
        out_specs=jax.tree.map(lambda _: vmem, out_shape),
        scratch_shapes=scratch,
        cost_estimate=cost,
        compiler_params=pltpu.CompilerParams(vmem_limit_bytes=VMEM_BYTES),
    )(*operands)


def pack_kernel(two_hbm, three_hbm, tensor_hbm, out_ref, tensor_ref, two_ref, three_ref, arrived):
    copies = [
        pltpu.make_async_copy(two_hbm, two_ref, arrived.at[0]),
        pltpu.make_async_copy(three_hbm, three_ref, arrived.at[1]),
    ]
    half = tensor_ref.shape[0] // 2
    for at in range(2):
        rows = pl.ds(at * half, half)
        copies.append(pltpu.make_async_copy(tensor_hbm.at[rows], tensor_ref.at[rows], arrived.at[2 + at]))
    for copy in reversed(copies):
        copy.start()
    for copy in copies[:2]:
        copy.wait()
    rank = two_ref.shape[-1]
    rows = [two_ref[0, r : r + 1, :] for r in range(two_ref.shape[1])]
    rows += [three_ref[0, r : r + 1, :] for r in range(three_ref.shape[1])]
    pieces, at = [], 0
    for slot, row in enumerate(rows):
        start = lane_start(slot, rank)
        if start > at:
            pieces.append(jnp.zeros((1, start - at), jnp.float32))
        pieces.append(row)
        at = start + rank
    pieces.append(jnp.zeros((1, out_ref.shape[-1] - at), jnp.float32))
    out_ref[...] = jnp.broadcast_to(jnp.concatenate(pieces, axis=1)[None], out_ref.shape)
    for copy in copies[2:]:
        copy.wait()


def parts_of(thrice, rank):
    high = thrice.astype(jnp.bfloat16).astype(jnp.float32)
    rest = thrice - high
    middle = rest.astype(jnp.bfloat16).astype(jnp.float32)
    lane = lax.broadcasted_iota(jnp.int32, thrice.shape, 1)
    return jnp.where(
        lane < rank, high, jnp.where(lane < 2 * rank, middle, rest - middle)
    ).astype(jnp.bfloat16)


def fold_lanes(wide, rank):
    return wide[:, :rank] + wide[:, rank : 2 * rank] + wide[:, 2 * rank : 3 * rank]


def fold_gram(full, rank):
    return fold_lanes(full[:rank] + full[rank : 2 * rank] + full[2 * rank : 3 * rank], rank)


def gram_of_parts(parts, rank):
    full = lax.dot_general(
        parts, parts, (((0,), (0,)), ((), ())), preferred_element_type=jnp.float32
    )
    return fold_gram(full, rank)


def contract_kernel(
    gathered_ref, tensor_ref, out_ref, two_ref, three_ref, sums_ref,
    gram_two_ref, gram_three_ref, *, rank, orders
):
    cores, chips = map(len, orders)
    count_two = two_ref.shape[0] // (cores * chips)
    count_three = three_ref.shape[0] // (cores * chips)
    half = chips // 2
    for at, core in enumerate(orders[0]):
        for first in range(0, chips, half):
            block = gathered_ref[at * chips + first : at * chips + first + half, :]
            chip = min(orders[1][first : first + half])
            turn = orders[1].index(chip) - first
            if turn:
                block = jnp.concatenate([block[turn:], block[:turn]], axis=0)
            for slot in range(count_two + count_three):
                start = lane_start(slot, rank)
                piece = block[:, start : start + rank]
                thrice = jnp.concatenate([piece, piece, piece], axis=1)
                ref, count, row = (
                    (two_ref, count_two, slot) if slot < count_two else (three_ref, count_three, slot - count_two)
                )
                row += count * (cores * chip + core)
                ref[pl.ds(row, half, stride=count * cores), :] = thrice
    two = two_ref[...]
    parts_three = parts_of(three_ref[...], rank)
    stacked = jnp.concatenate([parts_three, parts_three, parts_three], axis=0)
    for row in range(tensor_ref.shape[0]):
        cells = tensor_ref[row]
        high = cells.astype(jnp.bfloat16)
        rest = cells - high.astype(jnp.float32)
        middle = rest.astype(jnp.bfloat16)
        low = (rest - middle.astype(jnp.float32)).astype(jnp.bfloat16)
        through = jnp.dot(
            jnp.concatenate([high, middle, low], axis=1), stacked, preferred_element_type=jnp.float32
        )
        sums_ref[row : row + 1, :] = jnp.sum(through * two, axis=0, keepdims=True)
    partial = fold_lanes(sums_ref[...], rank).T
    gram_two_ref[...] = gram_of_parts(parts_of(two, rank), rank)
    gram_three_ref[...] = gram_of_parts(parts_three, rank)
    tiles = rank // SUBLANES
    tile_two = SUBLANES * jnp.minimum(lax.axis_index("ka"), tiles - 1)
    tile_three = SUBLANES * jnp.minimum(lax.axis_index("ja"), tiles - 1)
    pieces = [partial[SUBLANES * t : SUBLANES * (t + 1)] for t in range(tiles)]
    pieces.append(gram_two_ref[pl.ds(pl.multiple_of(tile_two, SUBLANES), SUBLANES), :])
    pieces.append(gram_three_ref[pl.ds(pl.multiple_of(tile_three, SUBLANES), SUBLANES), :])
    out_ref[...] = jnp.broadcast_to(jnp.concatenate(pieces, axis=1)[None], out_ref.shape)


def upper_spans(rank):
    return [(first, sum(rank - f for f in range(0, first, QUAD))) for first in range(0, rank, QUAD)]


def upper_width(rank):
    return sum(rank - first for first in range(0, rank, QUAD))


def upper_rows(full):
    rank = full.shape[0]
    return jnp.concatenate([full[f : f + QUAD, f:] for f, _ in upper_spans(rank)], axis=1)


def from_upper_rows(packed, rank):
    rows = []
    for first, at in upper_spans(rank):
        piece = packed[:, at : at + rank - first]
        rows.append(jnp.concatenate([jnp.zeros((QUAD, first), jnp.float32), piece], axis=1) if first else piece)
    upper = jnp.concatenate(rows, axis=0)
    down = lax.broadcasted_iota(jnp.int32, upper.shape, 0) // QUAD
    right = lax.broadcasted_iota(jnp.int32, upper.shape, 1) // QUAD
    return jnp.where(down > right, upper.T, upper)


def across_sublanes(tile, sublane):
    return jnp.broadcast_to(tile[sublane : sublane + 1, :], tile.shape)


def across_lanes(tile, lane):
    return jnp.broadcast_to(tile[:, lane : lane + 1], tile.shape)


def eliminate(tiles, rank):
    sublane = lax.broadcasted_iota(jnp.int32, tiles[0].shape, 0)

    def reduced(values, column, pivot_row, pivot_tile, pivot_sublane):
        out = [v - c * pivot_row for v, c in zip(values, column)]
        out[pivot_tile] = jnp.where(sublane == pivot_sublane, pivot_row, out[pivot_tile])
        return out

    for begin in range(0, rank, BLOCK):
        columns = [[across_lanes(v, begin + m) for v in tiles] for m in range(BLOCK)]
        pivot = across_sublanes(columns[0][begin // SUBLANES], begin % SUBLANES)
        for m in range(BLOCK):
            t, s = divmod(begin + m, SUBLANES)
            column = columns[m]
            inverse = 1.0 / pivot
            pivot_row = across_sublanes(tiles[t], s) * inverse
            if m + 1 < BLOCK:
                after = columns[m + 1]
                entry = across_sublanes(after[t], s) * inverse
                t_after, s_after = divmod(begin + m + 1, SUBLANES)
                pivot = across_sublanes(after[t_after], s_after)
                pivot -= across_sublanes(column[t_after], s_after) * entry
            tiles = reduced(tiles, column, pivot_row, t, s)
            for later in range(m + 1, BLOCK):
                entry = across_sublanes(columns[later][t], s) * inverse
                columns[later] = reduced(columns[later], column, entry, t, s)
    return tiles


def solve_kernel(parts_ref, out_ref, updated_ref, chip_ref, *, rank, rows, orders):
    tiles = rank // SUBLANES
    cores, groups_two, groups_three = map(len, orders)
    group = groups_two * groups_three
    place = {member: at for at, member in enumerate(itertools.product(*orders))}
    products = []
    for core in range(cores):
        first = place[core, orders[1][0], orders[2][0]]
        total = parts_ref[first]
        for source in range(1, group):
            total += parts_ref[first + source]
        products.append(total)
    at_two, at_three = tiles * rows, tiles * rows + rank
    augmented = []
    for t in range(tiles):
        gram_two = parts_ref[place[0, 0, t]]
        for j in range(1, groups_two):
            gram_two += parts_ref[place[0, j, t]]
        gram_three = parts_ref[place[0, t, 0]]
        for k in range(1, groups_three):
            gram_three += parts_ref[place[0, t, k]]
        system = gram_two[:, at_two : at_two + rank] * gram_three[:, at_three : at_three + rank]
        sides = [product[:, rows * t : rows * (t + 1)] for product in products]
        augmented.append(jnp.concatenate([system] + sides, axis=1))
    solved = jnp.concatenate([v[:, rank:] for v in eliminate(augmented, rank)], axis=0)
    chip_ref[...] = solved.T
    first = pl.multiple_of(rows * lax.axis_index("core"), SUBLANES)
    updated_ref[...] = chip_ref[pl.ds(first, rows), :]
    high = solved.astype(jnp.bfloat16)
    rest = solved - high.astype(jnp.float32)
    middle = rest.astype(jnp.bfloat16)
    low = (rest - middle.astype(jnp.float32)).astype(jnp.bfloat16)
    stacked = jnp.concatenate([high, middle, low], axis=0)
    full = lax.dot_general(
        stacked, stacked, (((1,), (1,)), ((), ())), preferred_element_type=jnp.float32
    )
    gram = fold_gram(full, rank)
    out_ref[...] = jnp.broadcast_to(upper_rows(gram)[None], out_ref.shape)


def scale_kernel(grams_ref, updated_ref, factor_ref, rms_ref, correlation_ref, *, rank, total_rows):
    total = grams_ref[0]
    for source in range(1, grams_ref.shape[0]):
        total += grams_ref[source]
    gram = from_upper_rows(total, rank)
    diagonal = jnp.where(
        lax.broadcasted_iota(jnp.int32, gram.shape, 0) == lax.broadcasted_iota(jnp.int32, gram.shape, 1),
        gram,
        0.0,
    )
    rms_row = jnp.sqrt(jnp.sum(diagonal, axis=0, keepdims=True) / total_rows + EPSILON)
    rms_column = jnp.sqrt(jnp.sum(diagonal, axis=1, keepdims=True) / total_rows + EPSILON)
    rms_ref[...] = rms_row
    factor_ref[...] = updated_ref[...] / rms_row
    correlation_ref[...] = gram / (rms_column * rms_row) / total_rows


def per_device(tensor, second_factor, third_factor):
    f32 = jnp.float32
    tensor, second_factor, third_factor = (
        pltpu.with_memory_space_constraint(v, pltpu.HBM) for v in (tensor, second_factor, third_factor)
    )
    rank = second_factor.shape[-1]
    chips, cores = lax.axis_size("z"), lax.axis_size("core")
    groups_two, groups_three = lax.axis_size("ja"), lax.axis_size("ka")
    members = chips * cores
    rows = tensor.shape[0]
    total_rows = rows * members
    slots = second_factor.shape[1] + third_factor.shape[1]
    width = -(-(lane_start(slots - 1, rank) + rank) // LANES) * LANES
    tiles = rank // SUBLANES

    packed, tensor = call(
        pack_kernel,
        (jax.ShapeDtypeStruct((members, 1, width), f32), jax.ShapeDtypeStruct(tensor.shape, f32)),
        [
            pltpu.VMEM(second_factor.shape, f32),
            pltpu.VMEM(third_factor.shape, f32),
            pltpu.SemaphoreType.DMA((4,)),
        ],
        second_factor,
        third_factor,
        tensor,
        fetched=(0, 1, 2),
    )
    cores_order = counted_from(cores - 1, cores)
    rows_order = (cores_order, upper_first(5 * chips // 8, chips))
    plane_order = (
        cores_order,
        counted_from(groups_two // 2, groups_two),
        counted_from(groups_three // 2, groups_three),
    )
    chips_order = (counted_from(chips // 2 + 1, chips),)
    gathered = exchange(packed, ("core", "z"), rows_order).reshape(members, width)

    messages = call(
        functools.partial(contract_kernel, rank=rank, orders=rows_order),
        jax.ShapeDtypeStruct((cores * groups_two * groups_three, SUBLANES, tiles * rows + 2 * rank), f32),
        [
            pltpu.VMEM((tensor.shape[1], 3 * rank), f32),
            pltpu.VMEM((tensor.shape[2], 3 * rank), f32),
            pltpu.VMEM((rows, 3 * rank), f32),
            pltpu.VMEM((rank, rank), f32),
            pltpu.VMEM((rank, rank), f32),
        ],
        gathered,
        tensor,
    )
    parts = exchange(messages, ("core", "ja", "ka"), plane_order)

    grams, updated = call(
        functools.partial(solve_kernel, rank=rank, rows=rows, orders=plane_order),
        (
            jax.ShapeDtypeStruct((chips, QUAD, upper_width(rank)), f32),
            jax.ShapeDtypeStruct((rows, rank), f32),
        ),
        [pltpu.VMEM((cores * rows, rank), f32)],
        parts,
    )
    grams = exchange(grams, ("z",), chips_order)

    factor, column_rms, correlation = call(
        functools.partial(scale_kernel, rank=rank, total_rows=total_rows),
        (
            jax.ShapeDtypeStruct((rows, rank), f32),
            jax.ShapeDtypeStruct((1, rank), f32),
            jax.ShapeDtypeStruct((rank, rank), f32),
        ),
        [],
        grams,
        updated,
    )
    return (factor, column_rms[0], correlation)


def solution(mesh):
    ia, ja, ka = (mesh.shape[name] for name in ("ia", "ja", "ka"))
    split = Mesh(mesh.devices.reshape(ia // 2, 2, ja, ka), ("z", "core", "ja", "ka"))
    first = ("z", "core")
    return jax.shard_map(
        per_device,
        mesh=split,
        in_specs=(P(first, "ja", "ka"), P("ja", first, None), P("ka", first, None)),
        out_specs=(P(first, None), P(), P()),
        check_vma=False,
    )
```

```python
import functools
import itertools

import jax
import jax.numpy as jnp
import numpy as np
from jax import lax
from jax.experimental import pallas as pl
from jax.experimental.pallas import tpu as pltpu
from jax.sharding import Mesh, PartitionSpec as P

EPSILON = 1e-06
LANES = 128
SUBLANES = 8
QUAD = 4
ROWS_AT_ONCE = 8
BLOCK = 12
VMEM_BYTES = 8 * 2**20


def counted_from(start, size):
    return [(start + step) % size for step in range(size)]


def upper_first(start, size):
    half = size // 2
    return [half + at for at in counted_from(start - half, half)] + list(range(half))


def exchange(copies, axes, orders):
    sizes = [lax.axis_size(axis) for axis in axes]
    listed = [int(np.ravel_multi_index(member, sizes)) for member in itertools.product(*orders)]
    return lax.all_to_all(copies, axes, 0, 0, tiled=True, axis_index_groups=[listed])


def lane_start(slot, rank):
    per_tile = LANES // rank
    return LANES * (slot // per_tile) + rank * (slot % per_tile)


def call(kernel, out_shape, scratch, *operands, fetched=(), cost=None):
    vmem, hbm = pl.BlockSpec(memory_space=pltpu.VMEM), pl.BlockSpec(memory_space=pltpu.HBM)
    return pl.pallas_call(
        kernel,
        out_shape=out_shape,
        in_specs=[hbm if at in fetched else vmem for at in range(len(operands))],
        out_specs=jax.tree.map(lambda _: vmem, out_shape),
        scratch_shapes=scratch,
        cost_estimate=cost,
        compiler_params=pltpu.CompilerParams(vmem_limit_bytes=VMEM_BYTES),
    )(*operands)


def pack_kernel(two_hbm, three_hbm, tensor_hbm, out_ref, tensor_ref, two_ref, three_ref, arrived):
    copies = [
        pltpu.make_async_copy(two_hbm, two_ref, arrived.at[0]),
        pltpu.make_async_copy(three_hbm, three_ref, arrived.at[1]),
    ]
    half = tensor_ref.shape[0] // 2
    for at in range(2):
        rows = pl.ds(at * half, half)
        copies.append(pltpu.make_async_copy(tensor_hbm.at[rows], tensor_ref.at[rows], arrived.at[2 + at]))
    for copy in reversed(copies):
        copy.start()
    for copy in copies[:2]:
        copy.wait()
    rank = two_ref.shape[-1]
    rows = [two_ref[0, r : r + 1, :] for r in range(two_ref.shape[1])]
    rows += [three_ref[0, r : r + 1, :] for r in range(three_ref.shape[1])]
    pieces, at = [], 0
    for slot, row in enumerate(rows):
        start = lane_start(slot, rank)
        if start > at:
            pieces.append(jnp.zeros((1, start - at), jnp.float32))
        pieces.append(row)
        at = start + rank
    pieces.append(jnp.zeros((1, out_ref.shape[-1] - at), jnp.float32))
    out_ref[...] = jnp.broadcast_to(jnp.concatenate(pieces, axis=1)[None], out_ref.shape)
    for copy in copies[2:]:
        copy.wait()


def parts_of(thrice, rank):
    high = thrice.astype(jnp.bfloat16).astype(jnp.float32)
    rest = thrice - high
    middle = rest.astype(jnp.bfloat16).astype(jnp.float32)
    lane = lax.broadcasted_iota(jnp.int32, thrice.shape, 1)
    return jnp.where(
        lane < rank, high, jnp.where(lane < 2 * rank, middle, rest - middle)
    ).astype(jnp.bfloat16)


def fold_lanes(wide, rank):
    return wide[:, :rank] + wide[:, rank : 2 * rank] + wide[:, 2 * rank : 3 * rank]


def fold_gram(full, rank):
    return fold_lanes(full[:rank] + full[rank : 2 * rank] + full[2 * rank : 3 * rank], rank)


def gram_of_parts(parts, rank):
    full = lax.dot_general(
        parts, parts, (((0,), (0,)), ((), ())), preferred_element_type=jnp.float32
    )
    return fold_gram(full, rank)


def contract_kernel(
    gathered_ref, tensor_ref, out_ref, two_ref, three_ref, sums_ref,
    gram_two_ref, gram_three_ref, *, rank, orders
):
    cores, chips = map(len, orders)
    count_two = two_ref.shape[0] // (cores * chips)
    count_three = three_ref.shape[0] // (cores * chips)
    half = chips // 2
    for at, core in enumerate(orders[0]):
        for first in range(0, chips, half):
            block = gathered_ref[at * chips + first : at * chips + first + half, :]
            chip = min(orders[1][first : first + half])
            turn = orders[1].index(chip) - first
            if turn:
                block = jnp.concatenate([block[turn:], block[:turn]], axis=0)
            for slot in range(count_two + count_three):
                start = lane_start(slot, rank)
                piece = block[:, start : start + rank]
                thrice = jnp.concatenate([piece, piece, piece], axis=1)
                ref, count, row = (
                    (two_ref, count_two, slot) if slot < count_two else (three_ref, count_three, slot - count_two)
                )
                row += count * (cores * chip + core)
                ref[pl.ds(row, half, stride=count * cores), :] = thrice
    two = two_ref[...]
    parts_three = parts_of(three_ref[...], rank)
    stacked = jnp.concatenate([parts_three, parts_three, parts_three], axis=0)
    for row in range(0, tensor_ref.shape[0], ROWS_AT_ONCE):
        cells = tensor_ref[row : row + ROWS_AT_ONCE].reshape(-1, tensor_ref.shape[2])
        high = cells.astype(jnp.bfloat16)
        rest = cells - high.astype(jnp.float32)
        middle = rest.astype(jnp.bfloat16)
        low = (rest - middle.astype(jnp.float32)).astype(jnp.bfloat16)
        through = jnp.dot(
            jnp.concatenate([high, middle, low], axis=1), stacked, preferred_element_type=jnp.float32
        ).reshape(ROWS_AT_ONCE, *two.shape)
        sums_ref[row : row + ROWS_AT_ONCE, :] = jnp.sum(through * two[None], axis=1)
    partial = fold_lanes(sums_ref[...], rank).T
    gram_two_ref[...] = gram_of_parts(parts_of(two, rank), rank)
    gram_three_ref[...] = gram_of_parts(parts_three, rank)
    tiles = rank // SUBLANES
    tile_two = SUBLANES * jnp.minimum(lax.axis_index("ka"), tiles - 1)
    tile_three = SUBLANES * jnp.minimum(lax.axis_index("ja"), tiles - 1)
    pieces = [partial[SUBLANES * t : SUBLANES * (t + 1)] for t in range(tiles)]
    pieces.append(gram_two_ref[pl.ds(pl.multiple_of(tile_two, SUBLANES), SUBLANES), :])
    pieces.append(gram_three_ref[pl.ds(pl.multiple_of(tile_three, SUBLANES), SUBLANES), :])
    out_ref[...] = jnp.broadcast_to(jnp.concatenate(pieces, axis=1)[None], out_ref.shape)


def upper_spans(rank):
    return [(first, sum(rank - f for f in range(0, first, QUAD))) for first in range(0, rank, QUAD)]


def upper_width(rank):
    return sum(rank - first for first in range(0, rank, QUAD))


def upper_rows(full):
    rank = full.shape[0]
    return jnp.concatenate([full[f : f + QUAD, f:] for f, _ in upper_spans(rank)], axis=1)


def from_upper_rows(packed, rank):
    rows = []
    for first, at in upper_spans(rank):
        piece = packed[:, at : at + rank - first]
        rows.append(jnp.concatenate([jnp.zeros((QUAD, first), jnp.float32), piece], axis=1) if first else piece)
    upper = jnp.concatenate(rows, axis=0)
    down = lax.broadcasted_iota(jnp.int32, upper.shape, 0) // QUAD
    right = lax.broadcasted_iota(jnp.int32, upper.shape, 1) // QUAD
    return jnp.where(down > right, upper.T, upper)


def across_sublanes(tile, sublane):
    return jnp.broadcast_to(tile[sublane : sublane + 1, :], tile.shape)


def across_lanes(tile, lane):
    return jnp.broadcast_to(tile[:, lane : lane + 1], tile.shape)


def eliminate(tiles, rank):
    sublane = lax.broadcasted_iota(jnp.int32, tiles[0].shape, 0)

    def reduced(values, column, pivot_row, pivot_tile, pivot_sublane):
        out = [v - c * pivot_row for v, c in zip(values, column)]
        out[pivot_tile] = jnp.where(sublane == pivot_sublane, pivot_row, out[pivot_tile])
        return out

    for begin in range(0, rank, BLOCK):
        columns = [[across_lanes(v, begin + m) for v in tiles] for m in range(BLOCK)]
        pivot = across_sublanes(columns[0][begin // SUBLANES], begin % SUBLANES)
        for m in range(BLOCK):
            t, s = divmod(begin + m, SUBLANES)
            column = columns[m]
            inverse = 1.0 / pivot
            pivot_row = across_sublanes(tiles[t], s) * inverse
            if m + 1 < BLOCK:
                after = columns[m + 1]
                entry = across_sublanes(after[t], s) * inverse
                t_after, s_after = divmod(begin + m + 1, SUBLANES)
                pivot = across_sublanes(after[t_after], s_after)
                pivot -= across_sublanes(column[t_after], s_after) * entry
            tiles = reduced(tiles, column, pivot_row, t, s)
            for later in range(m + 1, BLOCK):
                entry = across_sublanes(columns[later][t], s) * inverse
                columns[later] = reduced(columns[later], column, entry, t, s)
    return tiles


def solve_kernel(parts_ref, out_ref, updated_ref, chip_ref, *, rank, rows, orders):
    tiles = rank // SUBLANES
    cores, groups_two, groups_three = map(len, orders)
    group = groups_two * groups_three
    place = {member: at for at, member in enumerate(itertools.product(*orders))}
    products = []
    for core in range(cores):
        first = place[core, orders[1][0], orders[2][0]]
        total = parts_ref[first]
        for source in range(1, group):
            total += parts_ref[first + source]
        products.append(total)
    at_two, at_three = tiles * rows, tiles * rows + rank
    augmented = []
    for t in range(tiles):
        gram_two = parts_ref[place[0, 0, t]]
        for j in range(1, groups_two):
            gram_two += parts_ref[place[0, j, t]]
        gram_three = parts_ref[place[0, t, 0]]
        for k in range(1, groups_three):
            gram_three += parts_ref[place[0, t, k]]
        system = gram_two[:, at_two : at_two + rank] * gram_three[:, at_three : at_three + rank]
        sides = [product[:, rows * t : rows * (t + 1)] for product in products]
        augmented.append(jnp.concatenate([system] + sides, axis=1))
    solved = jnp.concatenate([v[:, rank:] for v in eliminate(augmented, rank)], axis=0)
    chip_ref[...] = solved.T
    first = pl.multiple_of(rows * lax.axis_index("core"), SUBLANES)
    updated_ref[...] = chip_ref[pl.ds(first, rows), :]
    high = solved.astype(jnp.bfloat16)
    rest = solved - high.astype(jnp.float32)
    middle = rest.astype(jnp.bfloat16)
    low = (rest - middle.astype(jnp.float32)).astype(jnp.bfloat16)
    stacked = jnp.concatenate([high, middle, low], axis=0)
    full = lax.dot_general(
        stacked, stacked, (((1,), (1,)), ((), ())), preferred_element_type=jnp.float32
    )
    gram = fold_gram(full, rank)
    out_ref[...] = jnp.broadcast_to(upper_rows(gram)[None], out_ref.shape)


def scale_kernel(grams_ref, updated_ref, factor_ref, rms_ref, correlation_ref, *, rank, total_rows):
    total = grams_ref[0]
    for source in range(1, grams_ref.shape[0]):
        total += grams_ref[source]
    gram = from_upper_rows(total, rank)
    diagonal = jnp.where(
        lax.broadcasted_iota(jnp.int32, gram.shape, 0) == lax.broadcasted_iota(jnp.int32, gram.shape, 1),
        gram,
        0.0,
    )
    rms_row = jnp.sqrt(jnp.sum(diagonal, axis=0, keepdims=True) / total_rows + EPSILON)
    rms_column = jnp.sqrt(jnp.sum(diagonal, axis=1, keepdims=True) / total_rows + EPSILON)
    rms_ref[...] = rms_row
    factor_ref[...] = updated_ref[...] / rms_row
    correlation_ref[...] = gram / (rms_column * rms_row) / total_rows


def per_device(tensor, second_factor, third_factor):
    f32 = jnp.float32
    tensor, second_factor, third_factor = (
        pltpu.with_memory_space_constraint(v, pltpu.HBM) for v in (tensor, second_factor, third_factor)
    )
    rank = second_factor.shape[-1]
    chips, cores = lax.axis_size("z"), lax.axis_size("core")
    groups_two, groups_three = lax.axis_size("ja"), lax.axis_size("ka")
    members = chips * cores
    rows = tensor.shape[0]
    total_rows = rows * members
    slots = second_factor.shape[1] + third_factor.shape[1]
    width = -(-(lane_start(slots - 1, rank) + rank) // LANES) * LANES
    tiles = rank // SUBLANES

    packed, tensor = call(
        pack_kernel,
        (jax.ShapeDtypeStruct((members, 1, width), f32), jax.ShapeDtypeStruct(tensor.shape, f32)),
        [
            pltpu.VMEM(second_factor.shape, f32),
            pltpu.VMEM(third_factor.shape, f32),
            pltpu.SemaphoreType.DMA((4,)),
        ],
        second_factor,
        third_factor,
        tensor,
        fetched=(0, 1, 2),
    )
    cores_order = counted_from(cores - 1, cores)
    rows_order = (cores_order, upper_first(5 * chips // 8, chips))
    plane_order = (
        cores_order,
        counted_from(groups_two // 2, groups_two),
        counted_from(groups_three // 2, groups_three),
    )
    chips_order = (counted_from(chips // 2 + 1, chips),)
    gathered = exchange(packed, ("core", "z"), rows_order).reshape(members, width)

    messages = call(
        functools.partial(contract_kernel, rank=rank, orders=rows_order),
        jax.ShapeDtypeStruct((cores * groups_two * groups_three, SUBLANES, tiles * rows + 2 * rank), f32),
        [
            pltpu.VMEM((tensor.shape[1], 3 * rank), f32),
            pltpu.VMEM((tensor.shape[2], 3 * rank), f32),
            pltpu.VMEM((rows, 3 * rank), f32),
            pltpu.VMEM((rank, rank), f32),
            pltpu.VMEM((rank, rank), f32),
        ],
        gathered,
        tensor,
    )
    parts = exchange(messages, ("core", "ja", "ka"), plane_order)

    grams, updated = call(
        functools.partial(solve_kernel, rank=rank, rows=rows, orders=plane_order),
        (
            jax.ShapeDtypeStruct((chips, QUAD, upper_width(rank)), f32),
            jax.ShapeDtypeStruct((rows, rank), f32),
        ),
        [pltpu.VMEM((cores * rows, rank), f32)],
        parts,
    )
    grams = exchange(grams, ("z",), chips_order)

    factor, column_rms, correlation = call(
        functools.partial(scale_kernel, rank=rank, total_rows=total_rows),
        (
            jax.ShapeDtypeStruct((rows, rank), f32),
            jax.ShapeDtypeStruct((1, rank), f32),
            jax.ShapeDtypeStruct((rank, rank), f32),
        ),
        [],
        grams,
        updated,
    )
    return (factor, column_rms[0], correlation)


def solution(mesh):
    ia, ja, ka = (mesh.shape[name] for name in ("ia", "ja", "ka"))
    split = Mesh(mesh.devices.reshape(ia // 2, 2, ja, ka), ("z", "core", "ja", "ka"))
    first = ("z", "core")
    return jax.shard_map(
        per_device,
        mesh=split,
        in_specs=(P(first, "ja", "ka"), P("ja", first, None), P("ka", first, None)),
        out_specs=(P(first, None), P(), P()),
        check_vma=False,
    )
```

```python
import functools
import itertools

import jax
import jax.numpy as jnp
import numpy as np
from jax import lax
from jax.experimental import pallas as pl
from jax.experimental.pallas import tpu as pltpu
from jax.sharding import Mesh, PartitionSpec as P

EPSILON = 1e-06
LANES = 128
SUBLANES = 8
QUAD = 4
ROWS_AT_ONCE = 16
BLOCK = 12
VMEM_BYTES = 8 * 2**20


def counted_from(start, size):
    return [(start + step) % size for step in range(size)]


def upper_first(start, size):
    half = size // 2
    return [half + at for at in counted_from(start - half, half)] + list(range(half))


def exchange(copies, axes, orders):
    sizes = [lax.axis_size(axis) for axis in axes]
    listed = [int(np.ravel_multi_index(member, sizes)) for member in itertools.product(*orders)]
    return lax.all_to_all(copies, axes, 0, 0, tiled=True, axis_index_groups=[listed])


def lane_start(slot, rank):
    per_tile = LANES // rank
    return LANES * (slot // per_tile) + rank * (slot % per_tile)


def call(kernel, out_shape, scratch, *operands, fetched=(), cost=None):
    vmem, hbm = pl.BlockSpec(memory_space=pltpu.VMEM), pl.BlockSpec(memory_space=pltpu.HBM)
    return pl.pallas_call(
        kernel,
        out_shape=out_shape,
        in_specs=[hbm if at in fetched else vmem for at in range(len(operands))],
        out_specs=jax.tree.map(lambda _: vmem, out_shape),
        scratch_shapes=scratch,
        cost_estimate=cost,
        compiler_params=pltpu.CompilerParams(vmem_limit_bytes=VMEM_BYTES),
    )(*operands)


def pack_kernel(two_hbm, three_hbm, tensor_hbm, out_ref, tensor_ref, two_ref, three_ref, arrived):
    copies = [
        pltpu.make_async_copy(two_hbm, two_ref, arrived.at[0]),
        pltpu.make_async_copy(three_hbm, three_ref, arrived.at[1]),
    ]
    half = tensor_ref.shape[0] // 2
    for at in range(2):
        rows = pl.ds(at * half, half)
        copies.append(pltpu.make_async_copy(tensor_hbm.at[rows], tensor_ref.at[rows], arrived.at[2 + at]))
    for copy in reversed(copies):
        copy.start()
    for copy in copies[:2]:
        copy.wait()
    rank = two_ref.shape[-1]
    rows = [two_ref[0, r : r + 1, :] for r in range(two_ref.shape[1])]
    rows += [three_ref[0, r : r + 1, :] for r in range(three_ref.shape[1])]
    pieces, at = [], 0
    for slot, row in enumerate(rows):
        start = lane_start(slot, rank)
        if start > at:
            pieces.append(jnp.zeros((1, start - at), jnp.float32))
        pieces.append(row)
        at = start + rank
    pieces.append(jnp.zeros((1, out_ref.shape[-1] - at), jnp.float32))
    out_ref[...] = jnp.broadcast_to(jnp.concatenate(pieces, axis=1)[None], out_ref.shape)
    for copy in copies[2:]:
        copy.wait()


def parts_of(thrice, rank):
    high = thrice.astype(jnp.bfloat16).astype(jnp.float32)
    rest = thrice - high
    middle = rest.astype(jnp.bfloat16).astype(jnp.float32)
    lane = lax.broadcasted_iota(jnp.int32, thrice.shape, 1)
    return jnp.where(
        lane < rank, high, jnp.where(lane < 2 * rank, middle, rest - middle)
    ).astype(jnp.bfloat16)


def fold_lanes(wide, rank):
    return wide[:, :rank] + wide[:, rank : 2 * rank] + wide[:, 2 * rank : 3 * rank]


def fold_gram(full, rank):
    return fold_lanes(full[:rank] + full[rank : 2 * rank] + full[2 * rank : 3 * rank], rank)


def gram_of_parts(parts, rank):
    full = lax.dot_general(
        parts, parts, (((0,), (0,)), ((), ())), preferred_element_type=jnp.float32
    )
    return fold_gram(full, rank)


def contract_kernel(
    gathered_ref, tensor_ref, out_ref, two_ref, three_ref, sums_ref,
    gram_two_ref, gram_three_ref, *, rank, orders
):
    cores, chips = map(len, orders)
    count_two = two_ref.shape[0] // (cores * chips)
    count_three = three_ref.shape[0] // (cores * chips)
    half = chips // 2
    for at, core in enumerate(orders[0]):
        for first in range(0, chips, half):
            block = gathered_ref[at * chips + first : at * chips + first + half, :]
            chip = min(orders[1][first : first + half])
            turn = orders[1].index(chip) - first
            if turn:
                block = jnp.concatenate([block[turn:], block[:turn]], axis=0)
            for slot in range(count_two + count_three):
                start = lane_start(slot, rank)
                piece = block[:, start : start + rank]
                thrice = jnp.concatenate([piece, piece, piece], axis=1)
                ref, count, row = (
                    (two_ref, count_two, slot) if slot < count_two else (three_ref, count_three, slot - count_two)
                )
                row += count * (cores * chip + core)
                ref[pl.ds(row, half, stride=count * cores), :] = thrice
    two = two_ref[...]
    parts_three = parts_of(three_ref[...], rank)
    stacked = jnp.concatenate([parts_three, parts_three, parts_three], axis=0)
    for row in range(0, tensor_ref.shape[0], ROWS_AT_ONCE):
        cells = tensor_ref[row : row + ROWS_AT_ONCE].reshape(-1, tensor_ref.shape[2])
        high = cells.astype(jnp.bfloat16)
        rest = cells - high.astype(jnp.float32)
        middle = rest.astype(jnp.bfloat16)
        low = (rest - middle.astype(jnp.float32)).astype(jnp.bfloat16)
        through = jnp.dot(
            jnp.concatenate([high, middle, low], axis=1), stacked, preferred_element_type=jnp.float32
        ).reshape(ROWS_AT_ONCE, *two.shape)
        sums_ref[row : row + ROWS_AT_ONCE, :] = jnp.sum(through * two[None], axis=1)
    partial = fold_lanes(sums_ref[...], rank).T
    gram_two_ref[...] = gram_of_parts(parts_of(two, rank), rank)
    gram_three_ref[...] = gram_of_parts(parts_three, rank)
    tiles = rank // SUBLANES
    tile_two = SUBLANES * jnp.minimum(lax.axis_index("ka"), tiles - 1)
    tile_three = SUBLANES * jnp.minimum(lax.axis_index("ja"), tiles - 1)
    pieces = [partial[SUBLANES * t : SUBLANES * (t + 1)] for t in range(tiles)]
    pieces.append(gram_two_ref[pl.ds(pl.multiple_of(tile_two, SUBLANES), SUBLANES), :])
    pieces.append(gram_three_ref[pl.ds(pl.multiple_of(tile_three, SUBLANES), SUBLANES), :])
    out_ref[...] = jnp.broadcast_to(jnp.concatenate(pieces, axis=1)[None], out_ref.shape)


def upper_spans(rank):
    return [(first, sum(rank - f for f in range(0, first, QUAD))) for first in range(0, rank, QUAD)]


def upper_width(rank):
    return sum(rank - first for first in range(0, rank, QUAD))


def upper_rows(full):
    rank = full.shape[0]
    return jnp.concatenate([full[f : f + QUAD, f:] for f, _ in upper_spans(rank)], axis=1)


def from_upper_rows(packed, rank):
    rows = []
    for first, at in upper_spans(rank):
        piece = packed[:, at : at + rank - first]
        rows.append(jnp.concatenate([jnp.zeros((QUAD, first), jnp.float32), piece], axis=1) if first else piece)
    upper = jnp.concatenate(rows, axis=0)
    down = lax.broadcasted_iota(jnp.int32, upper.shape, 0) // QUAD
    right = lax.broadcasted_iota(jnp.int32, upper.shape, 1) // QUAD
    return jnp.where(down > right, upper.T, upper)


def across_sublanes(tile, sublane):
    return jnp.broadcast_to(tile[sublane : sublane + 1, :], tile.shape)


def across_lanes(tile, lane):
    return jnp.broadcast_to(tile[:, lane : lane + 1], tile.shape)


def eliminate(tiles, rank):
    sublane = lax.broadcasted_iota(jnp.int32, tiles[0].shape, 0)

    def reduced(values, column, pivot_row, pivot_tile, pivot_sublane):
        out = [v - c * pivot_row for v, c in zip(values, column)]
        out[pivot_tile] = jnp.where(sublane == pivot_sublane, pivot_row, out[pivot_tile])
        return out

    for begin in range(0, rank, BLOCK):
        columns = [[across_lanes(v, begin + m) for v in tiles] for m in range(BLOCK)]
        pivot = across_sublanes(columns[0][begin // SUBLANES], begin % SUBLANES)
        for m in range(BLOCK):
            t, s = divmod(begin + m, SUBLANES)
            column = columns[m]
            inverse = 1.0 / pivot
            pivot_row = across_sublanes(tiles[t], s) * inverse
            if m + 1 < BLOCK:
                after = columns[m + 1]
                entry = across_sublanes(after[t], s) * inverse
                t_after, s_after = divmod(begin + m + 1, SUBLANES)
                pivot = across_sublanes(after[t_after], s_after)
                pivot -= across_sublanes(column[t_after], s_after) * entry
            tiles = reduced(tiles, column, pivot_row, t, s)
            for later in range(m + 1, BLOCK):
                entry = across_sublanes(columns[later][t], s) * inverse
                columns[later] = reduced(columns[later], column, entry, t, s)
    return tiles


def solve_kernel(parts_ref, out_ref, updated_ref, chip_ref, *, rank, rows, orders):
    tiles = rank // SUBLANES
    cores, groups_two, groups_three = map(len, orders)
    group = groups_two * groups_three
    place = {member: at for at, member in enumerate(itertools.product(*orders))}
    products = []
    for core in range(cores):
        first = place[core, orders[1][0], orders[2][0]]
        total = parts_ref[first]
        for source in range(1, group):
            total += parts_ref[first + source]
        products.append(total)
    at_two, at_three = tiles * rows, tiles * rows + rank
    augmented = []
    for t in range(tiles):
        gram_two = parts_ref[place[0, 0, t]]
        for j in range(1, groups_two):
            gram_two += parts_ref[place[0, j, t]]
        gram_three = parts_ref[place[0, t, 0]]
        for k in range(1, groups_three):
            gram_three += parts_ref[place[0, t, k]]
        system = gram_two[:, at_two : at_two + rank] * gram_three[:, at_three : at_three + rank]
        sides = [product[:, rows * t : rows * (t + 1)] for product in products]
        augmented.append(jnp.concatenate([system] + sides, axis=1))
    solved = jnp.concatenate([v[:, rank:] for v in eliminate(augmented, rank)], axis=0)
    chip_ref[...] = solved.T
    first = pl.multiple_of(rows * lax.axis_index("core"), SUBLANES)
    updated_ref[...] = chip_ref[pl.ds(first, rows), :]
    high = solved.astype(jnp.bfloat16)
    rest = solved - high.astype(jnp.float32)
    middle = rest.astype(jnp.bfloat16)
    low = (rest - middle.astype(jnp.float32)).astype(jnp.bfloat16)
    stacked = jnp.concatenate([high, middle, low], axis=0)
    full = lax.dot_general(
        stacked, stacked, (((1,), (1,)), ((), ())), preferred_element_type=jnp.float32
    )
    gram = fold_gram(full, rank)
    out_ref[...] = jnp.broadcast_to(upper_rows(gram)[None], out_ref.shape)


def scale_kernel(grams_ref, updated_ref, factor_ref, rms_ref, correlation_ref, *, rank, total_rows):
    total = grams_ref[0]
    for source in range(1, grams_ref.shape[0]):
        total += grams_ref[source]
    gram = from_upper_rows(total, rank)
    diagonal = jnp.where(
        lax.broadcasted_iota(jnp.int32, gram.shape, 0) == lax.broadcasted_iota(jnp.int32, gram.shape, 1),
        gram,
        0.0,
    )
    rms_row = jnp.sqrt(jnp.sum(diagonal, axis=0, keepdims=True) / total_rows + EPSILON)
    rms_column = jnp.sqrt(jnp.sum(diagonal, axis=1, keepdims=True) / total_rows + EPSILON)
    rms_ref[...] = rms_row
    factor_ref[...] = updated_ref[...] / rms_row
    correlation_ref[...] = gram / (rms_column * rms_row) / total_rows


def per_device(tensor, second_factor, third_factor):
    f32 = jnp.float32
    tensor, second_factor, third_factor = (
        pltpu.with_memory_space_constraint(v, pltpu.HBM) for v in (tensor, second_factor, third_factor)
    )
    rank = second_factor.shape[-1]
    chips, cores = lax.axis_size("z"), lax.axis_size("core")
    groups_two, groups_three = lax.axis_size("ja"), lax.axis_size("ka")
    members = chips * cores
    rows = tensor.shape[0]
    total_rows = rows * members
    slots = second_factor.shape[1] + third_factor.shape[1]
    width = -(-(lane_start(slots - 1, rank) + rank) // LANES) * LANES
    tiles = rank // SUBLANES

    packed, tensor = call(
        pack_kernel,
        (jax.ShapeDtypeStruct((members, 1, width), f32), jax.ShapeDtypeStruct(tensor.shape, f32)),
        [
            pltpu.VMEM(second_factor.shape, f32),
            pltpu.VMEM(third_factor.shape, f32),
            pltpu.SemaphoreType.DMA((4,)),
        ],
        second_factor,
        third_factor,
        tensor,
        fetched=(0, 1, 2),
    )
    cores_order = counted_from(cores - 1, cores)
    rows_order = (cores_order, upper_first(5 * chips // 8, chips))
    plane_order = (
        cores_order,
        counted_from(groups_two // 2, groups_two),
        counted_from(groups_three // 2, groups_three),
    )
    chips_order = (counted_from(chips // 2 + 1, chips),)
    gathered = exchange(packed, ("core", "z"), rows_order).reshape(members, width)

    messages = call(
        functools.partial(contract_kernel, rank=rank, orders=rows_order),
        jax.ShapeDtypeStruct((cores * groups_two * groups_three, SUBLANES, tiles * rows + 2 * rank), f32),
        [
            pltpu.VMEM((tensor.shape[1], 3 * rank), f32),
            pltpu.VMEM((tensor.shape[2], 3 * rank), f32),
            pltpu.VMEM((rows, 3 * rank), f32),
            pltpu.VMEM((rank, rank), f32),
            pltpu.VMEM((rank, rank), f32),
        ],
        gathered,
        tensor,
    )
    parts = exchange(messages, ("core", "ja", "ka"), plane_order)

    grams, updated = call(
        functools.partial(solve_kernel, rank=rank, rows=rows, orders=plane_order),
        (
            jax.ShapeDtypeStruct((chips, QUAD, upper_width(rank)), f32),
            jax.ShapeDtypeStruct((rows, rank), f32),
        ),
        [pltpu.VMEM((cores * rows, rank), f32)],
        parts,
    )
    grams = exchange(grams, ("z",), chips_order)

    factor, column_rms, correlation = call(
        functools.partial(scale_kernel, rank=rank, total_rows=total_rows),
        (
            jax.ShapeDtypeStruct((rows, rank), f32),
            jax.ShapeDtypeStruct((1, rank), f32),
            jax.ShapeDtypeStruct((rank, rank), f32),
        ),
        [],
        grams,
        updated,
    )
    return (factor, column_rms[0], correlation)


def solution(mesh):
    ia, ja, ka = (mesh.shape[name] for name in ("ia", "ja", "ka"))
    split = Mesh(mesh.devices.reshape(ia // 2, 2, ja, ka), ("z", "core", "ja", "ka"))
    first = ("z", "core")
    return jax.shard_map(
        per_device,
        mesh=split,
        in_specs=(P(first, "ja", "ka"), P("ja", first, None), P("ka", first, None)),
        out_specs=(P(first, None), P(), P()),
        check_vma=False,
    )
```
